32 devices in a mesh: groups: 1, row: 16 (over z, y, core), col: 2 (over x), rep: 1.
Axes of the slice: x: 2, y: 2, z: 4, core: 2. Of those that a mesh axis runs over, the one named last changes fastest.
Arguments:
- bins: bfloat16 [256, 1536], P(('groups', 'row', 'col')), may hold values from -6 to 6
- row_proj: bfloat16 [96, 1536], P('rep'), may hold values from -0.15625 to 0.15625
- col_proj: bfloat16 [96, 1536], P('rep'), may hold values from -0.15625 to 0.15625
- conv_weight: bfloat16 [3, 9, 96, 96], P(None, None, 'rep'), may hold values from -0.21875 to 0.21875
- conv_bias: float32 [3, 96], P(None, 'rep'), may hold values from -3 to 3
Outputs:
- contact_map: bfloat16 [96, 256, 256], P('rep', ('groups', 'row'), 'col')
The draws below stay inside these ranges and needn't reach their ends.
All inputs are finite; a program needn't handle non-finite values.
Results may differ from the reference program's by a relative error of at most 0.013.
Values may be sent and summed in bfloat16 or wider, within the bound.
A program may use at most 128 MiB of HBM per device.

```python
import jax
import jax.numpy as jnp
from jax import lax

E = 1536
C = 96
LAYERS = 3
BINS = 256


def level_of(stream_key, shape, shards, low, high):
    loudness, own = 1.0, jax.random.fold_in(stream_key, 6)
    for position, parts in shards:
        steps = jnp.exp(jax.random.uniform(jax.random.fold_in(own, position), (parts,), jnp.float32, low / len(shards), high / len(shards)))
        loudness = loudness * jnp.repeat(steps, shape[position] // parts).reshape([-1 if axis == position else 1 for axis in range(len(shape))])
    return loudness


def bell_draw(own_key, dims, width, bound, shards=(), held_as=jnp.bfloat16):
    factor_of = level_of(own_key, dims, shards, -0.22, 0.18) if shards else 1.0
    array = jax.random.normal(own_key, dims, jnp.float32) * width * factor_of
    return jnp.minimum(jnp.maximum(array, -bound), bound).astype(held_as)


def setup_inputs(seed: int = 0, part: int = 0) -> dict:
    key_list = jax.random.split(jax.random.key(seed), 6)
    own_keys = jax.random.split(jax.random.fold_in(key_list[5], part), 6)
    bins = bell_draw(own_keys[0], (BINS, E), 1.0, 6.0, ((0, 32),))
    row_proj = bell_draw(key_list[1], (C, E), E ** -0.5, 0.15625)
    col_proj = bell_draw(key_list[2], (C, E), E ** -0.5, 0.15625)
    conv_weight = bell_draw(key_list[3], (LAYERS, 9, C, C), (9 * C) ** -0.5, 0.21875)
    conv_bias = bell_draw(key_list[4], (LAYERS, C), 0.5, 3.0, (), jnp.float32)
    return dict(bins=bins, row_proj=row_proj, col_proj=col_proj, conv_weight=conv_weight, conv_bias=conv_bias)


def conv_layer(state, weights, bias, spread):
    active = jnp.maximum(state, 0).astype(jnp.float32)[None]
    channels_out = weights.shape[1]
    channels_in = weights.shape[2]
    kernel = weights.astype(jnp.float32).reshape(3, 3, channels_out, channels_in).transpose(2, 3, 0, 1)
    conv = lax.conv_general_dilated(active, kernel, (1, 1), [(spread, spread), (spread, spread)], rhs_dilation=(spread, spread), dimension_numbers=("NCHW", "OIHW", "NCHW"), precision=lax.Precision.HIGHEST)[0]
    return (state.astype(jnp.float32) + conv + bias.astype(jnp.float32)[:, None, None]).astype(jnp.bfloat16)


def reference(bins, row_proj, col_proj, conv_weight, conv_bias):
    row_terms = jnp.dot(bins, row_proj.T, preferred_element_type=jnp.float32).astype(jnp.bfloat16)
    col_terms = jnp.dot(bins, col_proj.T, preferred_element_type=jnp.float32).astype(jnp.bfloat16)
    state = (row_terms.T.astype(jnp.float32)[:, :, None] * col_terms.T.astype(jnp.float32)[:, None, :]).astype(jnp.bfloat16)
    state = conv_layer(state, conv_weight[0], conv_bias[0], 1)
    state = conv_layer(state, conv_weight[1], conv_bias[1], 2)
    widened = state.astype(jnp.float32)
    state = ((widened + widened.transpose(0, 2, 1)) * 0.5).astype(jnp.bfloat16)
    state = conv_layer(state, conv_weight[2], conv_bias[2], 4)
    return state
```

```python
import functools

import jax
import jax.numpy as jnp
from jax import lax
from jax.experimental import pallas as pl
from jax.experimental.pallas import tpu as pltpu
from jax.sharding import PartitionSpec as P

MESH = pl.DeviceIdType.MESH
EDGE = 8
LANES = 128
GROUP = 3 * LANES
WIDE = 4 * LANES
NT = (((1,), (1,)), ((), ()))


def gather_kernel(rows, cols, bins_ref, rp_ref, cp_ref, near_ref, far_ref, held, send_sem, recv_sem):
    count = rows * cols
    row_index = lax.axis_index("row")
    col_index = lax.axis_index("col")
    me = row_index * cols + col_index
    span, channels = bins_ref.shape[0], rp_ref.shape[0]

    def place(step):
        other = lax.rem(me + step, count)
        return {"row": lax.div(other, cols), "col": lax.rem(other, cols)}

    barrier = pltpu.get_barrier_semaphore()

    def greet(step, carry):
        pl.semaphore_signal(barrier, inc=1, device_id=place(step), device_id_type=MESH)
        return carry

    lax.fori_loop(1, count, greet, 0)
    bins = bins_ref[...]
    terms = [
        lax.dot_general(bins, ref[...], NT, preferred_element_type=jnp.float32)
        for ref in (rp_ref, cp_ref)
    ]
    block = jnp.concatenate(terms, axis=0)
    fill = jnp.zeros((2 * span, LANES - channels), jnp.float32)
    held[me] = jnp.concatenate([block, fill], axis=1).astype(jnp.bfloat16)
    near_ref[...] = jnp.zeros_like(near_ref)
    far_ref[...] = jnp.zeros_like(far_ref)
    pl.semaphore_wait(barrier, count - 1)

    def copy(step):
        return pltpu.make_async_remote_copy(
            src_ref=held.at[me],
            dst_ref=held.at[me],
            send_sem=send_sem.at[step],
            recv_sem=recv_sem.at[step],
            device_id=place(step),
            device_id_type=MESH,
        )

    def send(step, carry):
        copy(step).start()
        return carry

    def finish(step, carry):
        copy(step).wait()
        return carry

    lax.fori_loop(1, count, send, 0)
    lax.fori_loop(1, count, finish, 0)

    def lay(out_ref, first, blocks, offset):
        def one(index, carry):
            block_index = first + index

            @pl.when((block_index >= 0) & (block_index < count))
            def _():
                values = held[block_index].astype(jnp.float32)
                at = pl.ds(pl.multiple_of(offset + index * span, 8), span)
                out_ref[0, at, :] = values[:span]
                out_ref[1, at, :] = values[span:]

            return carry

        lax.fori_loop(0, blocks, one, 0)

    tile_rows = near_ref.shape[1] - 2 * EDGE
    tile_cols = far_ref.shape[1] - 4 * EDGE
    lay(near_ref, (row_index * tile_rows - EDGE) // span, (tile_rows + 2 * EDGE) // span, 0)
    lay(far_ref, (col_index * tile_cols - EDGE) // span, (tile_cols + 2 * EDGE) // span, EDGE)


def rounded(value):
    return value.astype(jnp.bfloat16).astype(jnp.float32)


def fill_filters(packed, slot, w_ref, layer, swapped, starts):
    channels = w_ref.shape[2]
    packed[slot] = jnp.zeros(packed.shape[1:], packed.dtype)
    for slab in range(4):
        for parity in range(2):
            first = slab - parity
            if 0 <= first <= 2:
                for second in range(3):
                    tap = 3 * second + first if swapped else 3 * first + second
                    lane = starts[slab] + second * LANES
                    packed[slot, parity * LANES : parity * LANES + channels, lane : lane + channels] = w_ref[
                        layer, tap
                    ]


def conv_kernel(total, near_ref, far_ref, w_ref, b_ref, out_ref, state, stacked, packed, result):
    channels, tile_rows, tile_cols = out_ref.shape
    pitch = tile_cols + 2 * EDGE
    frame = tile_rows + 2 * EDGE
    row_index = lax.axis_index("row")
    col_index = lax.axis_index("col")
    packs = (0, GROUP, 2 * GROUP, 3 * GROUP)
    last_packs = (0, GROUP, GROUP + WIDE, GROUP + 2 * WIDE)
    for layer in range(2):
        for swapped in range(2):
            fill_filters(packed, 2 * layer + swapped, w_ref, layer, swapped, packs)
    fill_filters(packed, 4, w_ref, 2, 0, last_packs)
    ones = (
        lax.broadcasted_iota(jnp.int32, (LANES, LANES), 0)
        == lax.broadcasted_iota(jnp.int32, (LANES, LANES), 1)
    ).astype(jnp.float32).astype(jnp.bfloat16)
    for parity in range(2):
        lane = last_packs[1 + parity] + GROUP
        packed[4, parity * LANES : (parity + 1) * LANES, lane : lane + LANES] = ones

    fill = jnp.zeros((1, LANES - channels), jnp.float32)
    biases = [jnp.concatenate([b_ref[l : l + 1, :], fill], axis=1) for l in range(3)]
    place = lax.broadcasted_iota(jnp.int32, (pitch, LANES), 0)
    low = jnp.maximum(EDGE - col_index * tile_cols, 0)
    high = jnp.minimum(pitch, total - col_index * tile_cols + EDGE)

    def masked(value, row):
        where = row_index * tile_rows - EDGE + row
        top = jnp.where((where >= 0) & (where < total), high, 0)
        return jnp.where((place >= low) & (place < top), value, 0.0)

    def at_row(row):
        return pl.ds(pl.multiple_of(EDGE + row * pitch, 8), pitch)

    base, spread = 2, 1
    groups = (frame - 2 * base) // (2 * spread)
    for side in range(2):
        for second in range(3):
            begin = EDGE + (second - 1) * spread
            shifted = far_ref[1 - side, begin : begin + pitch, :]

            def build(index, carry, side=side, second=second, shifted=shifted):
                for parity in range(2):
                    row = base - spread + 2 * index + parity
                    value = near_ref[side, pl.ds(row, 1), :] * shifted
                    at = pl.ds(pl.multiple_of(index * pitch, 16), pitch)
                    stacked[side, parity, at, second * LANES : (second + 1) * LANES] = jnp.maximum(
                        value, 0.0
                    ).astype(jnp.bfloat16)
                return carry

            lax.fori_loop(0, groups + 1, build, 0)

    def window(side, index, chunk):
        here = pl.ds(pl.multiple_of(index * chunk, 16), chunk)
        after = pl.ds(pl.multiple_of((index + 1) * chunk, 16), chunk)
        return jnp.concatenate(
            [stacked[side, p, at, :GROUP] for at in (here, after) for p in range(2)], axis=1
        )

    def first_layer(index, carry):
        for side in range(2):
            acc = lax.dot_general(
                window(side, index, pitch),
                packed[side, :, : 4 * GROUP],
                NT,
                preferred_element_type=jnp.float32,
            )
            for parity in range(2):
                row = base + 2 * index + parity
                old = near_ref[side, pl.ds(row, 1), :] * far_ref[1 - side, EDGE : EDGE + pitch, :]
                value = rounded(old) + acc[:, parity * LANES : (parity + 1) * LANES] + biases[0]
                state[side, at_row(row), :] = masked(rounded(value), row)
        return carry

    lax.fori_loop(0, groups, first_layer, 0)

    base1, spread1 = 4, 2
    groups1 = (frame - 2 * base1) // (2 * spread1)
    chunk1 = spread1 * pitch

    def build_second(index, carry):
        for side in range(2):
            for parity in range(2):
                for e in range(spread1):
                    row = base1 - spread1 + (2 * index + parity) * spread1 + e
                    at = pl.ds(pl.multiple_of(index * chunk1 + e * pitch, 16), pitch)
                    for second in range(3):
                        begin = EDGE + row * pitch + (second - 1) * spread1
                        value = jnp.maximum(state[side, pl.ds(begin, pitch), :], 0.0)
                        stacked[side, parity, at, second * LANES : (second + 1) * LANES] = value.astype(
                            jnp.bfloat16
                        )
        return carry

    lax.fori_loop(0, groups1 + 1, build_second, 0)

    def second_layer(index, carry):
        accs = [
            lax.dot_general(
                window(side, index, chunk1),
                packed[2 + side, :, : 4 * GROUP],
                NT,
                preferred_element_type=jnp.float32,
            )
            for side in range(2)
        ]
        for parity in range(2):
            for e in range(spread1):
                row = base1 + (2 * index + parity) * spread1 + e
                both = [
                    rounded(
                        state[side, at_row(row), :]
                        + accs[side][e * pitch : (e + 1) * pitch, parity * LANES : (parity + 1) * LANES]
                        + biases[1]
                    )
                    for side in range(2)
                ]
                state[0, at_row(row), :] = masked(rounded((both[0] + both[1]) * 0.5), row)
        return carry

    lax.fori_loop(0, groups1, second_layer, 0)

    base2, spread2 = EDGE, 4
    groups2 = tile_rows // (2 * spread2)
    chunk2 = spread2 * tile_cols

    def build_third(index, carry):
        for parity in range(2):
            for e in range(spread2):
                row = base2 - spread2 + (2 * index + parity) * spread2 + e
                at = pl.ds(pl.multiple_of(index * chunk2 + e * tile_cols, 16), tile_cols)
                for second in range(3):
                    begin = 2 * EDGE + row * pitch + (second - 1) * spread2
                    value = state[0, pl.ds(begin, tile_cols), :]
                    if second == 1:
                        stacked[0, parity, at, GROUP:] = value.astype(jnp.bfloat16)
                    stacked[0, parity, at, second * LANES : (second + 1) * LANES] = jnp.maximum(
                        value, 0.0
                    ).astype(jnp.bfloat16)
        return carry

    lax.fori_loop(0, groups2 + 1, build_third, 0)
    bias_rows = jnp.broadcast_to(biases[2], (LANES, LANES)).T[:channels]
    bias_rows = jnp.concatenate([bias_rows] * (tile_cols // LANES), axis=1)

    def third_layer(index, carry):
        here = pl.ds(pl.multiple_of(index * chunk2, 16), chunk2)
        after = pl.ds(pl.multiple_of((index + 1) * chunk2, 16), chunk2)
        pieces = [
            stacked[0, 0, here, :GROUP],
            stacked[0, 1, here, :],
            stacked[0, 0, after, :],
            stacked[0, 1, after, :GROUP],
        ]
        acc = lax.dot_general(
            packed[4], jnp.concatenate(pieces, axis=1), NT, preferred_element_type=jnp.float32
        )
        for parity in range(2):
            for e in range(spread2):
                row = (2 * index + parity) * spread2 + e
                value = (
                    acc[parity * LANES : parity * LANES + channels, e * tile_cols : (e + 1) * tile_cols]
                    + bias_rows
                )
                result[pl.ds(row, channels, stride=tile_rows), :] = value
        return carry

    lax.fori_loop(0, groups2, third_layer, 0)
    out_ref[...] = result[...].reshape(channels, tile_rows, tile_cols).astype(jnp.bfloat16)


def shards(bins, row_proj, col_proj, conv_weight, conv_bias):
    rows = lax.axis_size("row")
    cols = lax.axis_size("col")
    reps = lax.axis_size("rep")
    own = conv_bias.shape[1]
    if reps > 1:
        row_proj = lax.all_gather(row_proj, "rep", axis=0, tiled=True)
        col_proj = lax.all_gather(col_proj, "rep", axis=0, tiled=True)
        conv_weight = lax.all_gather(conv_weight, "rep", axis=2, tiled=True)
        conv_bias = lax.all_gather(conv_bias, "rep", axis=1, tiled=True)
    span = bins.shape[0]
    count = rows * cols
    total = span * count
    tile_rows = total // rows
    tile_cols = total // cols
    channels = conv_bias.shape[1]
    frame = tile_rows + 2 * EDGE
    pitch = tile_cols + 2 * EDGE
    vmem = pl.BlockSpec(memory_space=pltpu.VMEM)
    near, far = pl.pallas_call(
        functools.partial(gather_kernel, rows, cols),
        out_shape=[
            jax.ShapeDtypeStruct((2, frame, LANES), jnp.float32),
            jax.ShapeDtypeStruct((2, pitch + 2 * EDGE, LANES), jnp.float32),
        ],
        in_specs=[vmem] * 3,
        out_specs=[vmem] * 2,
        scratch_shapes=[
            pltpu.VMEM((count, 2 * span, LANES), jnp.bfloat16),
            pltpu.SemaphoreType.DMA((count,)),
            pltpu.SemaphoreType.DMA((count,)),
        ],
        compiler_params=pltpu.CompilerParams(
            collective_id=0, has_side_effects=True, vmem_limit_bytes=16 * 2**20
        ),
        name="gather_terms",
    )(bins, row_proj, col_proj)
    out = pl.pallas_call(
        functools.partial(conv_kernel, total),
        out_shape=jax.ShapeDtypeStruct((channels, tile_rows, tile_cols), jnp.bfloat16),
        in_specs=[vmem] * 4,
        out_specs=vmem,
        scratch_shapes=[
            pltpu.VMEM((2, frame * pitch + 2 * EDGE, LANES), jnp.float32),
            pltpu.VMEM((2, 2, frame // 2 * pitch, WIDE), jnp.bfloat16),
            pltpu.VMEM((5, 2 * LANES, 2 * GROUP + 2 * WIDE), jnp.bfloat16),
            pltpu.VMEM((channels * tile_rows, tile_cols), jnp.float32),
        ],
        compiler_params=pltpu.CompilerParams(vmem_limit_bytes=58 * 2**20),
        name="conv_stack",
    )(near, far, conv_weight, conv_bias)
    if reps > 1:
        out = lax.dynamic_slice_in_dim(out, lax.axis_index("rep") * own, own, 0)
    return out


def solution(mesh):
    placed = (
        P(("groups", "row", "col"), None),
        P("rep", None),
        P("rep", None),
        P(None, None, "rep", None),
        P(None, "rep"),
    )
    return jax.shard_map(
        shards,
        mesh=mesh,
        in_specs=placed,
        out_specs=P("rep", ("groups", "row"), "col"),
        check_vma=False,
    )
```

```python
import functools

import jax
import jax.numpy as jnp
from jax import lax
from jax.experimental import pallas as pl
from jax.experimental.pallas import tpu as pltpu
from jax.sharding import PartitionSpec as P

MESH = pl.DeviceIdType.MESH
EDGE = 8
LANES = 128
GROUP = 3 * LANES
PAIR = 2 * GROUP
NT = (((1,), (1,)), ((), ()))
ROWS_PER_DOT = 1024


def rounded(value):
    return value.astype(jnp.bfloat16).astype(jnp.float32)


def share(groups, chunk):
    return max(n for n in range(1, groups + 1) if groups % n == 0 and (n == 1 or n * chunk <= ROWS_PER_DOT))


def decoder(
    rows,
    cols,
    bins_hbm,
    rp_hbm,
    cp_hbm,
    w_hbm,
    b_hbm,
    out_ref,
    bins_ref,
    rp_ref,
    cp_ref,
    w_ref,
    b_ref,
    held,
    near_ref,
    far_ref,
    state,
    stacked,
    packed,
    result,
    load_sem,
    send_sem,
    recv_sem,
):
    count = rows * cols
    row_index = lax.axis_index("row")
    col_index = lax.axis_index("col")
    me = row_index * cols + col_index
    span, channels = bins_ref.shape[0], rp_ref.shape[0]
    total = span * count
    _, tile_rows, tile_cols = out_ref.shape
    pitch = tile_cols + 2 * EDGE
    frame = tile_rows + 2 * EDGE

    loads = [
        pltpu.make_async_copy(source, target, load_sem.at[i])
        for i, (source, target) in enumerate(
            [(bins_hbm, bins_ref), (rp_hbm, rp_ref), (cp_hbm, cp_ref), (w_hbm, w_ref), (b_hbm, b_ref)]
        )
    ]
    for load in loads:
        load.start()

    def uses(block, other):
        near_block = lax.div(other, cols) * (tile_rows // span)
        far_block = lax.rem(other, cols) * (tile_cols // span)
        return ((block >= near_block - 1) & (block <= near_block + tile_rows // span)) | (
            (block >= far_block - 1) & (block <= far_block + tile_cols // span)
        )

    def ahead(step):
        return lax.rem(me + step, count)

    def behind(step):
        return lax.rem(me + count - step, count)

    def place(other):
        return {"row": lax.div(other, cols), "col": lax.rem(other, cols)}

    barrier = pltpu.get_barrier_semaphore()

    def greet(step, targets):
        @pl.when(uses(behind(step), me))
        def _():
            pl.semaphore_signal(barrier, inc=1, device_id=place(behind(step)), device_id_type=MESH)

        return targets + jnp.where(uses(me, ahead(step)), 1, 0)

    targets = lax.fori_loop(1, count, greet, 0)
    for load in loads[:3]:
        load.wait()
    bins = bins_ref[...]
    terms = [
        lax.dot_general(bins, ref[...], NT, preferred_element_type=jnp.float32)
        for ref in (rp_ref, cp_ref)
    ]
    blank = jnp.zeros((2 * span, LANES - channels), jnp.float32)
    held[me] = jnp.concatenate([jnp.concatenate(terms, axis=0), blank], axis=1).astype(jnp.bfloat16)
    pl.semaphore_wait(barrier, targets)

    def copy(step):
        return pltpu.make_async_remote_copy(
            src_ref=held.at[me],
            dst_ref=held.at[me],
            send_sem=send_sem.at[step],
            recv_sem=recv_sem.at[step],
            device_id=place(ahead(step)),
            device_id_type=MESH,
        )

    def send(step, carry):
        @pl.when(uses(me, ahead(step)))
        def _():
            copy(step).start()

        return carry

    lax.fori_loop(1, count, send, 0)

    near_ref[...] = jnp.zeros_like(near_ref)
    far_ref[...] = jnp.zeros_like(far_ref)
    packed[...] = jnp.zeros_like(packed)
    for load in loads[3:]:
        load.wait()
    for layer in range(3):
        for tap in range(9):
            filters = w_ref[layer, tap].astype(jnp.float32).T.astype(jnp.bfloat16)
            for swapped in range(2 if layer < 2 else 1):
                first, second = (tap % 3, tap // 3) if swapped else (tap // 3, tap % 3)
                for parity in range(2):
                    at = (first + parity) * GROUP + second * LANES
                    packed[
                        2 * layer + swapped,
                        at : at + channels,
                        parity * LANES : parity * LANES + channels,
                    ] = filters
    fill = jnp.zeros((1, LANES - channels), jnp.float32)
    biases = [jnp.concatenate([b_ref[l : l + 1, :], fill], axis=1) for l in range(3)]

    def finish(step, carry):
        @pl.when(uses(behind(step), me))
        def _():
            copy(step).wait_recv()

        return carry

    lax.fori_loop(1, count, finish, 0)

    def lay(out, first, blocks, offset):
        def one(index, carry):
            block = first + index

            @pl.when((block >= 0) & (block < count))
            def _():
                values = held[block].astype(jnp.float32)
                at = pl.ds(pl.multiple_of(offset + index * span, 8), span)
                out[0, at, :] = values[:span]
                out[1, at, :] = values[span:]

            return carry

        lax.fori_loop(0, blocks, one, 0)

    lay(near_ref, row_index * (tile_rows // span) - 1, frame // span, 0)
    lay(far_ref, col_index * (tile_cols // span) - 1, pitch // span, EDGE)

    position = lax.broadcasted_iota(jnp.int32, (pitch, LANES), 0)
    low = jnp.maximum(EDGE - col_index * tile_cols, 0)
    high = jnp.minimum(pitch, total - col_index * tile_cols + EDGE)

    def masked(value, row):
        where = row_index * tile_rows - EDGE + row
        top = jnp.where((where >= 0) & (where < total), high, 0)
        return jnp.where((position >= low) & (position < top), value, 0.0)

    def at_row(row):
        return pl.ds(pl.multiple_of(EDGE + row * pitch, 8), pitch)

    def convolved(side, slot, index, n, chunk):
        here = pl.ds(pl.multiple_of(index * (n * chunk), 16), n * chunk)
        after = pl.ds(pl.multiple_of(index * (n * chunk) + chunk, 16), n * chunk)
        return jnp.dot(
            jnp.concatenate([stacked[side, here, :], stacked[side, after, :]], axis=1),
            packed[slot],
            preferred_element_type=jnp.float32,
        )

    def outputs(n, chunk, spread):
        width = chunk // spread
        for group in range(n):
            for parity in range(2):
                for e in range(spread):
                    begin = group * chunk + e * width
                    yield (
                        (2 * group + parity) * spread + e,
                        slice(begin, begin + width),
                        slice(parity * LANES, (parity + 1) * LANES),
                    )

    base = 2
    groups = (frame - 2 * base) // 2
    for side in range(2):
        for second in range(3):
            begin = EDGE + second - 1
            shifted = far_ref[1 - side, begin : begin + pitch, :]

            def build(index, carry, side=side, second=second, shifted=shifted):
                for parity in range(2):
                    value = near_ref[side, pl.ds(base - 1 + 2 * index + parity, 1), :] * shifted
                    at = pl.ds(pl.multiple_of(index * pitch, 16), pitch)
                    lane = parity * GROUP + second * LANES
                    stacked[side, at, lane : lane + LANES] = jnp.maximum(value, 0.0).astype(jnp.bfloat16)
                return carry

            lax.fori_loop(0, groups + 1, build, 0)
    n0 = share(groups, pitch)

    def first_layer(index, carry):
        for side in range(2):
            acc = convolved(side, side, index, n0, pitch)
            for step, pixels, lanes in outputs(n0, pitch, 1):
                row = base + 2 * n0 * index + step
                old = near_ref[side, pl.ds(row, 1), :] * far_ref[1 - side, EDGE : EDGE + pitch, :]
                value = rounded(old) + acc[pixels, lanes] + biases[0]
                state[side, at_row(row), :] = masked(rounded(value), row)
        return carry

    lax.fori_loop(0, groups // n0, first_layer, 0)

    base1, spread1 = 4, 2
    groups1 = (frame - 2 * base1) // (2 * spread1)
    chunk1 = spread1 * pitch

    def build_second(index, carry):
        for side in range(2):
            for parity in range(2):
                for e in range(spread1):
                    row = base1 - spread1 + (2 * index + parity) * spread1 + e
                    at = pl.ds(pl.multiple_of(index * chunk1 + e * pitch, 16), pitch)
                    for second in range(3):
                        begin = EDGE + row * pitch + (second - 1) * spread1
                        value = jnp.maximum(state[side, pl.ds(begin, pitch), :], 0.0)
                        lane = parity * GROUP + second * LANES
                        stacked[side, at, lane : lane + LANES] = value.astype(jnp.bfloat16)
        return carry

    lax.fori_loop(0, groups1 + 1, build_second, 0)
    n1 = share(groups1, chunk1)

    def second_layer(index, carry):
        accs = [convolved(side, 2 + side, index, n1, chunk1) for side in range(2)]
        for step, pixels, lanes in outputs(n1, chunk1, spread1):
            row = base1 + 2 * n1 * spread1 * index + step
            both = [
                rounded(state[side, at_row(row), :] + accs[side][pixels, lanes] + biases[1])
                for side in range(2)
            ]
            state[0, at_row(row), :] = masked(rounded((both[0] + both[1]) * 0.5), row)
        return carry

    lax.fori_loop(0, groups1 // n1, second_layer, 0)

    base2, spread2 = EDGE, 4
    groups2 = tile_rows // (2 * spread2)
    chunk2 = spread2 * tile_cols

    def build_third(index, carry):
        for parity in range(2):
            for e in range(spread2):
                row = base2 - spread2 + (2 * index + parity) * spread2 + e
                at = pl.ds(pl.multiple_of(index * chunk2 + e * tile_cols, 16), tile_cols)
                for second in range(3):
                    begin = 2 * EDGE + row * pitch + (second - 1) * spread2
                    value = jnp.maximum(state[0, pl.ds(begin, tile_cols), :], 0.0)
                    lane = parity * GROUP + second * LANES
                    stacked[0, at, lane : lane + LANES] = value.astype(jnp.bfloat16)
        return carry

    lax.fori_loop(0, groups2 + 1, build_third, 0)
    n2 = share(groups2, chunk2)

    def third_layer(index, carry):
        acc = convolved(0, 4, index, n2, chunk2)
        for step, pixels, lanes in outputs(n2, chunk2, spread2):
            row = 2 * n2 * spread2 * index + step
            begin = pl.multiple_of(2 * EDGE + (base2 + row) * pitch, 8)
            value = state[0, pl.ds(begin, tile_cols), :] + acc[pixels, lanes] + biases[2]
            result[pl.ds(row, channels, stride=tile_rows), :] = value.T[:channels]
        return carry

    lax.fori_loop(0, groups2 // n2, third_layer, 0)
    out_ref[...] = result[...].reshape(channels, tile_rows, tile_cols).astype(jnp.bfloat16)

    def sent(step, carry):
        @pl.when(uses(me, ahead(step)))
        def _():
            copy(step).wait_send()

        return carry

    lax.fori_loop(1, count, sent, 0)


def shards(bins, row_proj, col_proj, conv_weight, conv_bias):
    rows = lax.axis_size("row")
    cols = lax.axis_size("col")
    reps = lax.axis_size("rep")
    own = conv_bias.shape[1]
    if reps > 1:
        row_proj = lax.all_gather(row_proj, "rep", axis=0, tiled=True)
        col_proj = lax.all_gather(col_proj, "rep", axis=0, tiled=True)
        conv_weight = lax.all_gather(conv_weight, "rep", axis=2, tiled=True)
        conv_bias = lax.all_gather(conv_bias, "rep", axis=1, tiled=True)
    span = bins.shape[0]
    count = rows * cols
    total = span * count
    tile_rows = total // rows
    tile_cols = total // cols
    channels = conv_bias.shape[1]
    frame = tile_rows + 2 * EDGE
    pitch = tile_cols + 2 * EDGE
    operands = (bins, row_proj, col_proj, conv_weight, conv_bias)
    out = pl.pallas_call(
        functools.partial(decoder, rows, cols),
        out_shape=jax.ShapeDtypeStruct((channels, tile_rows, tile_cols), jnp.bfloat16),
        in_specs=[pl.BlockSpec(memory_space=pltpu.MemorySpace.HBM)] * 5,
        out_specs=pl.BlockSpec(memory_space=pltpu.VMEM),
        scratch_shapes=[pltpu.VMEM(x.shape, x.dtype) for x in operands]
        + [
            pltpu.VMEM((count, 2 * span, LANES), jnp.bfloat16),
            pltpu.VMEM((2, frame, LANES), jnp.float32),
            pltpu.VMEM((2, pitch + 2 * EDGE, LANES), jnp.float32),
            pltpu.VMEM((2, frame * pitch + 2 * EDGE, LANES), jnp.float32),
            pltpu.VMEM((2, frame // 2 * pitch, PAIR), jnp.bfloat16),
            pltpu.VMEM((5, 2 * PAIR, 2 * LANES), jnp.bfloat16),
            pltpu.VMEM((channels * tile_rows, tile_cols), jnp.float32),
            pltpu.SemaphoreType.DMA((5,)),
            pltpu.SemaphoreType.DMA((count,)),
            pltpu.SemaphoreType.DMA((count,)),
        ],
        compiler_params=pltpu.CompilerParams(
            collective_id=0, has_side_effects=True, vmem_limit_bytes=60 * 2**20
        ),
        name="decode_map",
    )(*operands)
    if reps > 1:
        out = lax.dynamic_slice_in_dim(out, lax.axis_index("rep") * own, own, 0)
    return out


def solution(mesh):
    placed = (
        P(("groups", "row", "col"), None),
        P("rep", None),
        P("rep", None),
        P(None, None, "rep", None),
        P(None, "rep"),
    )
    return jax.shard_map(
        shards,
        mesh=mesh,
        in_specs=placed,
        out_specs=P("rep", ("groups", "row"), "col"),
        check_vma=False,
    )
```

```python
import functools

import jax
import jax.numpy as jnp
from jax import lax
from jax.experimental import pallas as pl
from jax.experimental.pallas import tpu as pltpu
from jax.sharding import PartitionSpec as P

MESH = pl.DeviceIdType.MESH
EDGE = 8
LANES = 128
GROUP = 3 * LANES
PAIR = 2 * GROUP
NT = (((1,), (1,)), ((), ()))
ROWS_PER_DOT = 512
MOST_CHUNKS = 16
SPARE = 24 * 2**20


def rounded(value):
    return value.astype(jnp.bfloat16).astype(jnp.float32)


def share(groups, chunk):
    return max(n for n in range(1, groups + 1) if groups % n == 0 and (n == 1 or n * chunk <= ROWS_PER_DOT))


def decoder(
    rows,
    cols,
    bins_hbm,
    rp_hbm,
    cp_hbm,
    w_hbm,
    b_hbm,
    out_ref,
    bins_ref,
    rp_ref,
    cp_ref,
    w_ref,
    b_ref,
    held,
    near_ref,
    far_ref,
    state,
    stacked,
    packed,
    result,
    load_sem,
    send_sem,
    recv_sem,
):
    count = rows * cols
    row_index = lax.axis_index("row")
    col_index = lax.axis_index("col")
    me = row_index * cols + col_index
    span, channels = bins_ref.shape[0], rp_ref.shape[0]
    total = span * count
    _, tile_rows, tile_cols = out_ref.shape
    pitch = tile_cols + 2 * EDGE
    frame = tile_rows + 2 * EDGE
    apart = stacked.shape[0] - 2

    loads = [
        pltpu.make_async_copy(source, target, load_sem.at[i])
        for i, (source, target) in enumerate(
            [(bins_hbm, bins_ref), (rp_hbm, rp_ref), (cp_hbm, cp_ref), (w_hbm, w_ref), (b_hbm, b_ref)]
        )
    ]
    for load in loads:
        load.start()

    def uses(block, other):
        near_block = lax.div(other, cols) * (tile_rows // span)
        far_block = lax.rem(other, cols) * (tile_cols // span)
        return ((block >= near_block - 1) & (block <= near_block + tile_rows // span)) | (
            (block >= far_block - 1) & (block <= far_block + tile_cols // span)
        )

    def ahead(step):
        return lax.rem(me + step, count)

    def behind(step):
        return lax.rem(me + count - step, count)

    def place(other):
        return {"row": lax.div(other, cols), "col": lax.rem(other, cols)}

    barrier = pltpu.get_barrier_semaphore()

    def greet(step, targets):
        @pl.when(uses(behind(step), me))
        def _():
            pl.semaphore_signal(barrier, inc=1, device_id=place(behind(step)), device_id_type=MESH)

        return targets + jnp.where(uses(me, ahead(step)), 1, 0)

    targets = lax.fori_loop(1, count, greet, 0)
    near_ref[...] = jnp.zeros_like(near_ref)
    far_ref[...] = jnp.zeros_like(far_ref)
    packed[...] = jnp.zeros_like(packed)
    for load in loads[:3]:
        load.wait()
    bins = bins_ref[...]
    terms = [
        lax.dot_general(bins, ref[...], NT, preferred_element_type=jnp.float32)
        for ref in (rp_ref, cp_ref)
    ]
    blank = jnp.zeros((2 * span, LANES - channels), jnp.float32)
    held[me] = jnp.concatenate([jnp.concatenate(terms, axis=0), blank], axis=1).astype(jnp.bfloat16)
    pl.semaphore_wait(barrier, targets)

    def copy(step):
        return pltpu.make_async_remote_copy(
            src_ref=held.at[me],
            dst_ref=held.at[me],
            send_sem=send_sem.at[step],
            recv_sem=recv_sem.at[step],
            device_id=place(ahead(step)),
            device_id_type=MESH,
        )

    def send(step, carry):
        @pl.when(uses(me, ahead(step)))
        def _():
            copy(step).start()

        return carry

    lax.fori_loop(1, count, send, 0)

    for load in loads[3:]:
        load.wait()
    for layer in range(3):
        for tap in range(9):
            filters = w_ref[layer, tap].astype(jnp.float32).T.astype(jnp.bfloat16)
            for swapped in range(2 if layer < 2 else 1):
                first, second = (tap % 3, tap // 3) if swapped else (tap // 3, tap % 3)
                for parity in range(2):
                    at = (first + parity) * GROUP + second * LANES
                    packed[
                        2 * layer + swapped,
                        at : at + channels,
                        parity * LANES : parity * LANES + channels,
                    ] = filters
    fill = jnp.zeros((1, LANES - channels), jnp.float32)
    biases = [jnp.concatenate([b_ref[l : l + 1, :], fill], axis=1) for l in range(3)]

    def finish(step, carry):
        @pl.when(uses(behind(step), me))
        def _():
            copy(step).wait_recv()

        return carry

    lax.fori_loop(1, count, finish, 0)

    def lay(out, first, blocks, offset):
        def one(index, carry):
            block = first + index

            @pl.when((block >= 0) & (block < count))
            def _():
                values = held[block].astype(jnp.float32)
                at = pl.ds(pl.multiple_of(offset + index * span, 8), span)
                out[0, at, :] = values[:span]
                out[1, at, :] = values[span:]

            return carry

        lax.fori_loop(0, blocks, one, 0)

    lay(near_ref, row_index * (tile_rows // span) - 1, frame // span, 0)
    lay(far_ref, col_index * (tile_cols // span) - 1, pitch // span, EDGE)

    cells = lax.broadcasted_iota(jnp.int32, (pitch, LANES), 0)
    edge_cells = cells[:EDGE]
    from_left = jnp.where(col_index > 0, 0, EDGE)
    to_right = jnp.where(col_index < cols - 1, EDGE, 0)
    from_top = jnp.where(row_index > 0, 0, pitch)
    from_bottom = jnp.where(row_index < rows - 1, 0, pitch)

    def masked(value, row):
        left = jnp.where(edge_cells >= from_left, value[:EDGE], 0.0)
        right = jnp.where(edge_cells < to_right, value[-EDGE:], 0.0)
        value = jnp.concatenate([left, value[EDGE:-EDGE], right], axis=0)
        if isinstance(row, int):
            if row < EDGE:
                value = jnp.where(cells >= from_top, value, 0.0)
            elif row >= EDGE + tile_rows:
                value = jnp.where(cells >= from_bottom, value, 0.0)
            return value
        start = jnp.where(row < EDGE, from_top, jnp.where(row >= EDGE + tile_rows, from_bottom, 0))
        return jnp.where(cells >= start, value, 0.0)

    def span_of(begin, size, unit=16):
        return pl.ds(begin if isinstance(begin, int) else pl.multiple_of(begin, unit), size)

    def at_row(row):
        return span_of(EDGE + row * pitch, pitch, 8)

    def convolved(side, slot, index, n, chunk):
        here = span_of(index * (n * chunk), n * chunk)
        after = span_of(index * (n * chunk) + chunk, n * chunk)
        return jnp.dot(
            jnp.concatenate([stacked[side, here, :], stacked[side, after, :]], axis=1),
            packed[slot],
            preferred_element_type=jnp.float32,
        )

    def outputs(n, chunk, spread):
        width = chunk // spread
        for group in range(n):
            for parity in range(2):
                for e in range(spread):
                    begin = group * chunk + e * width
                    yield (
                        (2 * group + parity) * spread + e,
                        slice(begin, begin + width),
                        slice(parity * LANES, (parity + 1) * LANES),
                    )

    def pipeline(groups, n, build, multiply, store):
        chunks = groups // n
        if chunks > MOST_CHUNKS:
            lax.fori_loop(0, groups + 1, lambda i, c: (build(i), c)[1], 0)
            lax.fori_loop(0, chunks, lambda i, c: (store(i, multiply(i)), c)[1], 0)
            return
        for i in range(n + 1):
            build(i)
        held_acc = None
        for i in range(chunks):
            acc = multiply(i)
            if i + 1 < chunks:
                for j in range(n):
                    build((i + 1) * n + 1 + j)
            if held_acc is not None:
                store(i - 1, held_acc)
            held_acc = acc
        store(chunks - 1, held_acc)

    base = 2
    groups = (frame - 2 * base) // 2
    n0 = share(groups, pitch)
    halves = pitch // 16
    shifted = [
        [
            far_ref[1 - side, EDGE + second - 1 : EDGE + second - 1 + pitch, :]
            .astype(jnp.bfloat16)
            .reshape(halves, 16, LANES)
            for second in range(3)
        ]
        for side in range(2)
    ]

    def product(side, row, second):
        line = jnp.broadcast_to(near_ref[side, pl.ds(row, 1), :], (16, LANES)).astype(jnp.bfloat16)
        return (line[None] * shifted[side][second]).reshape(pitch, LANES)

    def build_first(index):
        for side in range(2):
            for parity in range(2):
                for second in range(3):
                    value = product(side, base - 1 + 2 * index + parity, second)
                    lane = parity * GROUP + second * LANES
                    stacked[side, span_of(index * pitch, pitch), lane : lane + LANES] = jnp.maximum(
                        value, jnp.zeros_like(value)
                    )

    def store_first(index, accs):
        for side in range(2):
            for step, pixels, lanes in outputs(n0, pitch, 1):
                row = base + 2 * n0 * index + step
                old = product(side, row, 1).astype(jnp.float32)
                value = old + accs[side][pixels, lanes] + biases[0]
                state[side, at_row(row), :] = masked(rounded(value), row)

    pipeline(
        groups,
        n0,
        build_first,
        lambda index: [convolved(side, side, index, n0, pitch) for side in range(2)],
        store_first,
    )

    base1, spread1 = 4, 2
    groups1 = (frame - 2 * base1) // (2 * spread1)
    chunk1 = spread1 * pitch
    n1 = share(groups1, chunk1)

    def build_second(index):
        for side in range(2):
            for parity in range(2):
                for e in range(spread1):
                    row = base1 - spread1 + (2 * index + parity) * spread1 + e
                    at = span_of(index * chunk1 + e * pitch, pitch)
                    for second in range(3):
                        begin = EDGE + row * pitch + (second - 1) * spread1
                        value = jnp.maximum(state[side, pl.ds(begin, pitch), :], 0.0)
                        lane = parity * GROUP + second * LANES
                        stacked[apart + side, at, lane : lane + LANES] = value.astype(jnp.bfloat16)

    def store_second(index, accs):
        for step, pixels, lanes in outputs(n1, chunk1, spread1):
            row = base1 + 2 * n1 * spread1 * index + step
            both = [
                rounded(state[side, at_row(row), :] + accs[side][pixels, lanes] + biases[1])
                for side in range(2)
            ]
            state[2, at_row(row), :] = masked(rounded((both[0] + both[1]) * 0.5), row)

    pipeline(
        groups1,
        n1,
        build_second,
        lambda index: [convolved(apart + side, 2 + side, index, n1, chunk1) for side in range(2)],
        store_second,
    )

    base2, spread2 = EDGE, 4
    groups2 = tile_rows // (2 * spread2)
    chunk2 = spread2 * tile_cols
    n2 = share(groups2, chunk2)

    def build_third(index):
        for parity in range(2):
            for e in range(spread2):
                row = base2 - spread2 + (2 * index + parity) * spread2 + e
                at = span_of(index * chunk2 + e * tile_cols, tile_cols)
                for second in range(3):
                    begin = 2 * EDGE + row * pitch + (second - 1) * spread2
                    value = jnp.maximum(state[2, pl.ds(begin, tile_cols), :], 0.0)
                    lane = parity * GROUP + second * LANES
                    stacked[0, at, lane : lane + LANES] = value.astype(jnp.bfloat16)

    def store_third(index, acc):
        for step, pixels, lanes in outputs(n2, chunk2, spread2):
            row = 2 * n2 * spread2 * index + step
            begin = span_of(2 * EDGE + (base2 + row) * pitch, tile_cols, 8)
            value = state[2, begin, :] + acc[pixels, lanes] + biases[2]
            result[pl.ds(row, channels, stride=tile_rows), :] = value.T[:channels]

    pipeline(groups2, n2, build_third, lambda index: convolved(0, 4, index, n2, chunk2), store_third)
    out_ref[...] = result[...].reshape(channels, tile_rows, tile_cols).astype(jnp.bfloat16)

    def sent(step, carry):
        @pl.when(uses(me, ahead(step)))
        def _():
            copy(step).wait_send()

        return carry

    lax.fori_loop(1, count, sent, 0)


def shards(bins, row_proj, col_proj, conv_weight, conv_bias):
    rows = lax.axis_size("row")
    cols = lax.axis_size("col")
    reps = lax.axis_size("rep")
    own = conv_bias.shape[1]
    if reps > 1:
        row_proj = lax.all_gather(row_proj, "rep", axis=0, tiled=True)
        col_proj = lax.all_gather(col_proj, "rep", axis=0, tiled=True)
        conv_weight = lax.all_gather(conv_weight, "rep", axis=2, tiled=True)
        conv_bias = lax.all_gather(conv_bias, "rep", axis=1, tiled=True)
    span = bins.shape[0]
    count = rows * cols
    total = span * count
    tile_rows = total // rows
    tile_cols = total // cols
    channels = conv_bias.shape[1]
    frame = tile_rows + 2 * EDGE
    pitch = tile_cols + 2 * EDGE
    stack = frame // 2 * pitch * PAIR * 2
    operands = (bins, row_proj, col_proj, conv_weight, conv_bias)
    out = pl.pallas_call(
        functools.partial(decoder, rows, cols),
        out_shape=jax.ShapeDtypeStruct((channels, tile_rows, tile_cols), jnp.bfloat16),
        in_specs=[pl.BlockSpec(memory_space=pltpu.MemorySpace.HBM)] * 5,
        out_specs=pl.BlockSpec(memory_space=pltpu.VMEM),
        scratch_shapes=[pltpu.VMEM(x.shape, x.dtype) for x in operands]
        + [
            pltpu.VMEM((count, 2 * span, LANES), jnp.bfloat16),
            pltpu.VMEM((2, frame, LANES), jnp.float32),
            pltpu.VMEM((2, pitch + 2 * EDGE, LANES), jnp.float32),
            pltpu.VMEM((3, frame * pitch + 2 * EDGE, LANES), jnp.float32),
            pltpu.VMEM((4 if 4 * stack <= SPARE else 2, frame // 2 * pitch, PAIR), jnp.bfloat16),
            pltpu.VMEM((5, 2 * PAIR, 2 * LANES), jnp.bfloat16),
            pltpu.VMEM((channels * tile_rows, tile_cols), jnp.float32),
            pltpu.SemaphoreType.DMA((5,)),
            pltpu.SemaphoreType.DMA((count,)),
            pltpu.SemaphoreType.DMA((count,)),
        ],
        compiler_params=pltpu.CompilerParams(
            collective_id=0, has_side_effects=True, vmem_limit_bytes=60 * 2**20
        ),
        name="decode_map",
    )(*operands)
    if reps > 1:
        out = lax.dynamic_slice_in_dim(out, lax.axis_index("rep") * own, own, 0)
    return out


def solution(mesh):
    placed = (
        P(("groups", "row", "col"), None),
        P("rep", None),
        P("rep", None),
        P(None, None, "rep", None),
        P(None, "rep"),
    )
    return jax.shard_map(
        shards,
        mesh=mesh,
        in_specs=placed,
        out_specs=P("rep", ("groups", "row"), "col"),
        check_vma=False,
    )
```

```python
import functools

import jax
import jax.numpy as jnp
from jax import lax
from jax.experimental import pallas as pl
from jax.experimental.pallas import tpu as pltpu
from jax.sharding import PartitionSpec as P

MESH = pl.DeviceIdType.MESH
EDGE = 8
LANES = 128
GROUP = 3 * LANES
PAIR = 2 * GROUP
NT = (((1,), (1,)), ((), ()))
ROWS_PER_DOT = 1024
MOST_CHUNKS = 16
SPARE = 24 * 2**20


def rounded(value):
    return value.astype(jnp.bfloat16).astype(jnp.float32)


def share(groups, chunk):
    return max(n for n in range(1, groups + 1) if groups % n == 0 and (n == 1 or n * chunk <= ROWS_PER_DOT))


def decoder(
    rows,
    cols,
    bins_hbm,
    rp_hbm,
    cp_hbm,
    w_hbm,
    b_hbm,
    out_ref,
    bins_ref,
    rp_ref,
    cp_ref,
    w_ref,
    b_ref,
    held,
    near_ref,
    far_ref,
    state,
    stacked,
    packed,
    result,
    load_sem,
    send_sem,
    recv_sem,
):
    count = rows * cols
    row_index = lax.axis_index("row")
    col_index = lax.axis_index("col")
    me = row_index * cols + col_index
    span, channels = bins_ref.shape[0], rp_ref.shape[0]
    total = span * count
    _, tile_rows, tile_cols = out_ref.shape
    pitch = tile_cols + 2 * EDGE
    frame = tile_rows + 2 * EDGE
    apart = stacked.shape[0] - 2

    loads = [
        pltpu.make_async_copy(source, target, load_sem.at[i])
        for i, (source, target) in enumerate(
            [(bins_hbm, bins_ref), (rp_hbm, rp_ref), (cp_hbm, cp_ref), (w_hbm, w_ref), (b_hbm, b_ref)]
        )
    ]
    for load in loads:
        load.start()

    def uses(block, other):
        near_block = lax.div(other, cols) * (tile_rows // span)
        far_block = lax.rem(other, cols) * (tile_cols // span)
        return ((block >= near_block - 1) & (block <= near_block + tile_rows // span)) | (
            (block >= far_block - 1) & (block <= far_block + tile_cols // span)
        )

    def ahead(step):
        return lax.rem(me + step, count)

    def behind(step):
        return lax.rem(me + count - step, count)

    def place(other):
        return {"row": lax.div(other, cols), "col": lax.rem(other, cols)}

    barrier = pltpu.get_barrier_semaphore()

    def greet(step, targets):
        @pl.when(uses(behind(step), me))
        def _():
            pl.semaphore_signal(barrier, inc=1, device_id=place(behind(step)), device_id_type=MESH)

        return targets + jnp.where(uses(me, ahead(step)), 1, 0)

    targets = lax.fori_loop(1, count, greet, 0)
    near_ref[...] = jnp.zeros_like(near_ref)
    far_ref[...] = jnp.zeros_like(far_ref)
    packed[...] = jnp.zeros_like(packed)
    for load in loads[:3]:
        load.wait()
    bins = bins_ref[...]
    terms = [
        lax.dot_general(bins, ref[...], NT, preferred_element_type=jnp.float32)
        for ref in (rp_ref, cp_ref)
    ]
    blank = jnp.zeros((2 * span, LANES - channels), jnp.float32)
    held[me] = jnp.concatenate([jnp.concatenate(terms, axis=0), blank], axis=1).astype(jnp.bfloat16)
    pl.semaphore_wait(barrier, targets)

    def copy(step):
        return pltpu.make_async_remote_copy(
            src_ref=held.at[me],
            dst_ref=held.at[me],
            send_sem=send_sem.at[step],
            recv_sem=recv_sem.at[step],
            device_id=place(ahead(step)),
            device_id_type=MESH,
        )

    def send(step, carry):
        @pl.when(uses(me, ahead(step)))
        def _():
            copy(step).start()

        return carry

    lax.fori_loop(1, count, send, 0)

    for load in loads[3:]:
        load.wait()
    for layer in range(3):
        for tap in range(9):
            filters = w_ref[layer, tap].astype(jnp.float32).T.astype(jnp.bfloat16)
            for swapped in range(2 if layer < 2 else 1):
                first, second = (tap % 3, tap // 3) if swapped else (tap // 3, tap % 3)
                for parity in range(2):
                    at = (first + parity) * GROUP + second * LANES
                    packed[
                        2 * layer + swapped,
                        at : at + channels,
                        parity * LANES : parity * LANES + channels,
                    ] = filters
    fill = jnp.zeros((1, LANES - channels), jnp.float32)
    biases = [jnp.concatenate([b_ref[l : l + 1, :], fill], axis=1) for l in range(3)]

    def finish(step, carry):
        @pl.when(uses(behind(step), me))
        def _():
            copy(step).wait_recv()

        return carry

    lax.fori_loop(1, count, finish, 0)

    def lay(out, first, blocks, offset):
        def one(index, carry):
            block = first + index

            @pl.when((block >= 0) & (block < count))
            def _():
                values = held[block].astype(jnp.float32)
                at = pl.ds(pl.multiple_of(offset + index * span, 8), span)
                out[0, at, :] = values[:span]
                out[1, at, :] = values[span:]

            return carry

        lax.fori_loop(0, blocks, one, 0)

    lay(near_ref, row_index * (tile_rows // span) - 1, frame // span, 0)
    lay(far_ref, col_index * (tile_cols // span) - 1, pitch // span, EDGE)

    cells = lax.broadcasted_iota(jnp.int32, (pitch, LANES), 0)
    edge_cells = cells[:EDGE]
    from_left = jnp.where(col_index > 0, 0, EDGE)
    to_right = jnp.where(col_index < cols - 1, EDGE, 0)
    from_top = jnp.where(row_index > 0, 0, pitch)
    from_bottom = jnp.where(row_index < rows - 1, 0, pitch)

    def masked(value, row):
        left = jnp.where(edge_cells >= from_left, value[:EDGE], 0.0)
        right = jnp.where(edge_cells < to_right, value[-EDGE:], 0.0)
        value = jnp.concatenate([left, value[EDGE:-EDGE], right], axis=0)
        if isinstance(row, int):
            if row < EDGE:
                value = jnp.where(cells >= from_top, value, 0.0)
            elif row >= EDGE + tile_rows:
                value = jnp.where(cells >= from_bottom, value, 0.0)
            return value
        start = jnp.where(row < EDGE, from_top, jnp.where(row >= EDGE + tile_rows, from_bottom, 0))
        return jnp.where(cells >= start, value, 0.0)

    def span_of(begin, size, unit=16):
        return pl.ds(begin if isinstance(begin, int) else pl.multiple_of(begin, unit), size)

    def at_row(row):
        return span_of(EDGE + row * pitch, pitch, 8)

    def convolved(side, slot, index, n, chunk):
        here = span_of(index * (n * chunk), n * chunk)
        after = span_of(index * (n * chunk) + chunk, n * chunk)
        return jnp.dot(
            jnp.concatenate([stacked[side, here, :], stacked[side, after, :]], axis=1),
            packed[slot],
            preferred_element_type=jnp.float32,
        )

    def outputs(n, chunk, spread):
        width = chunk // spread
        for group in range(n):
            for parity in range(2):
                for e in range(spread):
                    begin = group * chunk + e * width
                    yield (
                        (2 * group + parity) * spread + e,
                        slice(begin, begin + width),
                        slice(parity * LANES, (parity + 1) * LANES),
                    )

    def pipeline(groups, n, build, multiply, store):
        chunks = groups // n
        if chunks > MOST_CHUNKS:
            lax.fori_loop(0, groups + 1, lambda i, c: (build(i), c)[1], 0)
            lax.fori_loop(0, chunks, lambda i, c: (store(i, multiply(i)), c)[1], 0)
            return
        for i in range(n + 1):
            build(i)
        held_acc = None
        for i in range(chunks):
            acc = multiply(i)
            if i + 1 < chunks:
                for j in range(n):
                    build((i + 1) * n + 1 + j)
            if held_acc is not None:
                store(i - 1, held_acc)
            held_acc = acc
        store(chunks - 1, held_acc)

    base = 2
    groups = (frame - 2 * base) // 2
    n0 = share(groups, pitch)
    halves = pitch // 16
    shifted = [
        [
            far_ref[1 - side, EDGE + second - 1 : EDGE + second - 1 + pitch, :]
            .astype(jnp.bfloat16)
            .reshape(halves, 16, LANES)
            for second in range(3)
        ]
        for side in range(2)
    ]

    def product(side, row, second):
        line = jnp.broadcast_to(near_ref[side, pl.ds(row, 1), :], (16, LANES)).astype(jnp.bfloat16)
        return (line[None] * shifted[side][second]).reshape(pitch, LANES)

    def build_first(index):
        for side in range(2):
            for parity in range(2):
                for second in range(3):
                    value = product(side, base - 1 + 2 * index + parity, second)
                    lane = parity * GROUP + second * LANES
                    stacked[side, span_of(index * pitch, pitch), lane : lane + LANES] = jnp.maximum(
                        value, jnp.zeros_like(value)
                    )

    def store_first(index, accs):
        for side in range(2):
            for step, pixels, lanes in outputs(n0, pitch, 1):
                row = base + 2 * n0 * index + step
                old = product(side, row, 1).astype(jnp.float32)
                value = old + accs[side][pixels, lanes] + biases[0]
                state[side, at_row(row), :] = masked(rounded(value), row)

    pipeline(
        groups,
        n0,
        build_first,
        lambda index: [convolved(side, side, index, n0, pitch) for side in range(2)],
        store_first,
    )

    base1, spread1 = 4, 2
    groups1 = (frame - 2 * base1) // (2 * spread1)
    chunk1 = spread1 * pitch
    n1 = share(groups1, chunk1)

    def build_second(index):
        for side in range(2):
            for parity in range(2):
                for e in range(spread1):
                    row = base1 - spread1 + (2 * index + parity) * spread1 + e
                    at = span_of(index * chunk1 + e * pitch, pitch)
                    for second in range(3):
                        begin = EDGE + row * pitch + (second - 1) * spread1
                        value = jnp.maximum(state[side, pl.ds(begin, pitch), :], 0.0)
                        lane = parity * GROUP + second * LANES
                        stacked[apart + side, at, lane : lane + LANES] = value.astype(jnp.bfloat16)

    def store_second(index, accs):
        for step, pixels, lanes in outputs(n1, chunk1, spread1):
            row = base1 + 2 * n1 * spread1 * index + step
            both = [
                rounded(state[side, at_row(row), :] + accs[side][pixels, lanes] + biases[1])
                for side in range(2)
            ]
            state[2, at_row(row), :] = masked(rounded((both[0] + both[1]) * 0.5), row)

    pipeline(
        groups1,
        n1,
        build_second,
        lambda index: [convolved(apart + side, 2 + side, index, n1, chunk1) for side in range(2)],
        store_second,
    )

    base2, spread2 = EDGE, 4
    groups2 = tile_rows // (2 * spread2)
    chunk2 = spread2 * tile_cols
    n2 = share(groups2, chunk2)

    def build_third(index):
        for parity in range(2):
            for e in range(spread2):
                row = base2 - spread2 + (2 * index + parity) * spread2 + e
                at = span_of(index * chunk2 + e * tile_cols, tile_cols)
                for second in range(3):
                    begin = 2 * EDGE + row * pitch + (second - 1) * spread2
                    value = jnp.maximum(state[2, pl.ds(begin, tile_cols), :], 0.0)
                    lane = parity * GROUP + second * LANES
                    stacked[0, at, lane : lane + LANES] = value.astype(jnp.bfloat16)

    def store_third(index, acc):
        for step, pixels, lanes in outputs(n2, chunk2, spread2):
            row = 2 * n2 * spread2 * index + step
            begin = span_of(2 * EDGE + (base2 + row) * pitch, tile_cols, 8)
            value = state[2, begin, :] + acc[pixels, lanes] + biases[2]
            result[pl.ds(row, channels, stride=tile_rows), :] = value.T[:channels]

    pipeline(groups2, n2, build_third, lambda index: convolved(0, 4, index, n2, chunk2), store_third)
    out_ref[...] = result[...].reshape(channels, tile_rows, tile_cols).astype(jnp.bfloat16)

    def sent(step, carry):
        @pl.when(uses(me, ahead(step)))
        def _():
            copy(step).wait_send()

        return carry

    lax.fori_loop(1, count, sent, 0)


def shards(bins, row_proj, col_proj, conv_weight, conv_bias):
    rows = lax.axis_size("row")
    cols = lax.axis_size("col")
    reps = lax.axis_size("rep")
    own = conv_bias.shape[1]
    if reps > 1:
        row_proj = lax.all_gather(row_proj, "rep", axis=0, tiled=True)
        col_proj = lax.all_gather(col_proj, "rep", axis=0, tiled=True)
        conv_weight = lax.all_gather(conv_weight, "rep", axis=2, tiled=True)
        conv_bias = lax.all_gather(conv_bias, "rep", axis=1, tiled=True)
    span = bins.shape[0]
    count = rows * cols
    total = span * count
    tile_rows = total // rows
    tile_cols = total // cols
    channels = conv_bias.shape[1]
    frame = tile_rows + 2 * EDGE
    pitch = tile_cols + 2 * EDGE
    stack = frame // 2 * pitch * PAIR * 2
    operands = (bins, row_proj, col_proj, conv_weight, conv_bias)
    out = pl.pallas_call(
        functools.partial(decoder, rows, cols),
        out_shape=jax.ShapeDtypeStruct((channels, tile_rows, tile_cols), jnp.bfloat16),
        in_specs=[pl.BlockSpec(memory_space=pltpu.MemorySpace.HBM)] * 5,
        out_specs=pl.BlockSpec(memory_space=pltpu.VMEM),
        scratch_shapes=[pltpu.VMEM(x.shape, x.dtype) for x in operands]
        + [
            pltpu.VMEM((count, 2 * span, LANES), jnp.bfloat16),
            pltpu.VMEM((2, frame, LANES), jnp.float32),
            pltpu.VMEM((2, pitch + 2 * EDGE, LANES), jnp.float32),
            pltpu.VMEM((3, frame * pitch + 2 * EDGE, LANES), jnp.float32),
            pltpu.VMEM((4 if 4 * stack <= SPARE else 2, frame // 2 * pitch, PAIR), jnp.bfloat16),
            pltpu.VMEM((5, 2 * PAIR, 2 * LANES), jnp.bfloat16),
            pltpu.VMEM((channels * tile_rows, tile_cols), jnp.float32),
            pltpu.SemaphoreType.DMA((5,)),
            pltpu.SemaphoreType.DMA((count,)),
            pltpu.SemaphoreType.DMA((count,)),
        ],
        compiler_params=pltpu.CompilerParams(
            collective_id=0, has_side_effects=True, vmem_limit_bytes=60 * 2**20
        ),
        name="decode_map",
    )(*operands)
    if reps > 1:
        out = lax.dynamic_slice_in_dim(out, lax.axis_index("rep") * own, own, 0)
    return out


def solution(mesh):
    placed = (
        P(("groups", "row", "col"), None),
        P("rep", None),
        P("rep", None),
        P(None, None, "rep", None),
        P(None, "rep"),
    )
    return jax.shard_map(
        shards,
        mesh=mesh,
        in_specs=placed,
        out_specs=P("rep", ("groups", "row"), "col"),
        check_vma=False,
    )
```

```python
import functools

import jax
import jax.numpy as jnp
from jax import lax
from jax.experimental import pallas as pl
from jax.experimental.pallas import tpu as pltpu
from jax.sharding import PartitionSpec as P

MESH = pl.DeviceIdType.MESH
EDGE = 8
LANES = 128
GROUP = 3 * LANES
PAIR = 2 * GROUP
NT = (((1,), (1,)), ((), ()))
ROWS_PER_DOT = 512
MOST_CHUNKS = 16
SPARE = 24 * 2**20


def rounded(value):
    return value.astype(jnp.bfloat16).astype(jnp.float32)


def share(groups, chunk):
    return max(n for n in range(1, groups + 1) if groups % n == 0 and (n == 1 or n * chunk <= ROWS_PER_DOT))


def decoder(
    rows,
    cols,
    bins_hbm,
    rp_hbm,
    cp_hbm,
    w_hbm,
    b_hbm,
    out_ref,
    bins_ref,
    rp_ref,
    cp_ref,
    w_ref,
    b_ref,
    held,
    near_ref,
    far_ref,
    state,
    stacked,
    packed,
    result,
    load_sem,
    send_sem,
    recv_sem,
):
    count = rows * cols
    row_index = lax.axis_index("row")
    col_index = lax.axis_index("col")
    me = row_index * cols + col_index
    span, channels = bins_ref.shape[0], rp_ref.shape[0]
    total = span * count
    _, tile_rows, tile_cols = out_ref.shape
    pitch = tile_cols + 2 * EDGE
    frame = tile_rows + 2 * EDGE
    apart = stacked.shape[0] - 2

    loads = [
        pltpu.make_async_copy(source, target, load_sem.at[i])
        for i, (source, target) in enumerate(
            [(bins_hbm, bins_ref), (rp_hbm, rp_ref), (cp_hbm, cp_ref), (w_hbm, w_ref), (b_hbm, b_ref)]
        )
    ]
    for load in loads:
        load.start()

    def uses(block, other):
        near_block = lax.div(other, cols) * (tile_rows // span)
        far_block = lax.rem(other, cols) * (tile_cols // span)
        return ((block >= near_block - 1) & (block <= near_block + tile_rows // span)) | (
            (block >= far_block - 1) & (block <= far_block + tile_cols // span)
        )

    def ahead(step):
        return lax.rem(me + step, count)

    def behind(step):
        return lax.rem(me + count - step, count)

    def place(other):
        return {"row": lax.div(other, cols), "col": lax.rem(other, cols)}

    barrier = pltpu.get_barrier_semaphore()

    def greet(step, targets):
        @pl.when(uses(behind(step), me))
        def _():
            pl.semaphore_signal(barrier, inc=1, device_id=place(behind(step)), device_id_type=MESH)

        return targets + jnp.where(uses(me, ahead(step)), 1, 0)

    targets = lax.fori_loop(1, count, greet, 0)
    near_ref[...] = jnp.zeros_like(near_ref)
    far_ref[...] = jnp.zeros_like(far_ref)
    packed[...] = jnp.zeros_like(packed)
    for load in loads[:3]:
        load.wait()
    bins = bins_ref[...]
    terms = [
        lax.dot_general(bins, ref[...], NT, preferred_element_type=jnp.float32)
        for ref in (rp_ref, cp_ref)
    ]
    blank = jnp.zeros((2 * span, LANES - channels), jnp.float32)
    held[me] = jnp.concatenate([jnp.concatenate(terms, axis=0), blank], axis=1).astype(jnp.bfloat16)
    pl.semaphore_wait(barrier, targets)

    def copy(step):
        return pltpu.make_async_remote_copy(
            src_ref=held.at[me],
            dst_ref=held.at[me],
            send_sem=send_sem.at[step],
            recv_sem=recv_sem.at[step],
            device_id=place(ahead(step)),
            device_id_type=MESH,
        )

    def send(step, carry):
        @pl.when(uses(me, ahead(step)))
        def _():
            copy(step).start()

        return carry

    lax.fori_loop(1, count, send, 0)

    for load in loads[3:]:
        load.wait()
    def pack(layer, tap):
        filters = w_ref[layer, tap].astype(jnp.float32).T.astype(jnp.bfloat16)
        for swapped in range(2 if layer < 2 else 1):
            first, second = (tap % 3, tap // 3) if swapped else (tap // 3, tap % 3)
            for parity in range(2):
                at = (first + parity) * GROUP + second * LANES
                packed[
                    2 * layer + swapped,
                    at : at + channels,
                    parity * LANES : parity * LANES + channels,
                ] = filters

    for tap in range(9):
        pack(0, tap)
    fill = jnp.zeros((1, LANES - channels), jnp.float32)
    biases = [jnp.concatenate([b_ref[l : l + 1, :], fill], axis=1) for l in range(3)]

    def finish(step, carry):
        @pl.when(uses(behind(step), me))
        def _():
            copy(step).wait_recv()

        return carry

    lax.fori_loop(1, count, finish, 0)

    def lay(out, first, blocks, offset):
        def one(index, carry):
            block = first + index

            @pl.when((block >= 0) & (block < count))
            def _():
                values = held[block].astype(jnp.float32)
                at = pl.ds(pl.multiple_of(offset + index * span, 8), span)
                out[0, at, :] = values[:span]
                out[1, at, :] = values[span:]

            return carry

        lax.fori_loop(0, blocks, one, 0)

    lay(near_ref, row_index * (tile_rows // span) - 1, frame // span, 0)
    lay(far_ref, col_index * (tile_cols // span) - 1, pitch // span, EDGE)

    cells = lax.broadcasted_iota(jnp.int32, (pitch, LANES), 0)
    edge_cells = cells[:EDGE]
    from_left = jnp.where(col_index > 0, 0, EDGE)
    to_right = jnp.where(col_index < cols - 1, EDGE, 0)
    from_top = jnp.where(row_index > 0, 0, pitch)
    from_bottom = jnp.where(row_index < rows - 1, 0, pitch)

    def masked(value, row):
        left = jnp.where(edge_cells >= from_left, value[:EDGE], 0.0)
        right = jnp.where(edge_cells < to_right, value[-EDGE:], 0.0)
        value = jnp.concatenate([left, value[EDGE:-EDGE], right], axis=0)
        if isinstance(row, int):
            if row < EDGE:
                value = jnp.where(cells >= from_top, value, 0.0)
            elif row >= EDGE + tile_rows:
                value = jnp.where(cells >= from_bottom, value, 0.0)
            return value
        start = jnp.where(row < EDGE, from_top, jnp.where(row >= EDGE + tile_rows, from_bottom, 0))
        return jnp.where(cells >= start, value, 0.0)

    def span_of(begin, size, unit=16):
        return pl.ds(begin if isinstance(begin, int) else pl.multiple_of(begin, unit), size)

    def at_row(row):
        return span_of(EDGE + row * pitch, pitch, 8)

    def convolved(side, slot, index, n, chunk):
        here = span_of(index * (n * chunk), n * chunk)
        after = span_of(index * (n * chunk) + chunk, n * chunk)
        return jnp.dot(
            jnp.concatenate([stacked[side, here, :], stacked[side, after, :]], axis=1),
            packed[slot],
            preferred_element_type=jnp.float32,
        )

    def outputs(n, chunk, spread):
        width = chunk // spread
        for group in range(n):
            for parity in range(2):
                for e in range(spread):
                    begin = group * chunk + e * width
                    yield (
                        (2 * group + parity) * spread + e,
                        slice(begin, begin + width),
                        slice(parity * LANES, (parity + 1) * LANES),
                    )

    def pipeline(groups, n, build, multiply, store, later):
        chunks = groups // n
        pending = [(later, tap) for tap in range(9)] if later < 3 else []
        quota = -(-len(pending) // chunks)
        if chunks > MOST_CHUNKS:
            for item in pending:
                pack(*item)
            lax.fori_loop(0, groups + 1, lambda i, c: (build(i), c)[1], 0)
            lax.fori_loop(0, chunks, lambda i, c: (store(i, multiply(i)), c)[1], 0)
            return
        for i in range(n + 1):
            build(i)
        held_acc = None
        for i in range(chunks):
            acc = multiply(i)
            for item in pending[i * quota : (i + 1) * quota]:
                pack(*item)
            if i + 1 < chunks:
                for j in range(n):
                    build((i + 1) * n + 1 + j)
            if held_acc is not None:
                store(i - 1, held_acc)
            held_acc = acc
        store(chunks - 1, held_acc)

    base = 2
    groups = (frame - 2 * base) // 2
    n0 = share(groups, pitch)
    halves = pitch // 16
    shifted = [
        [
            far_ref[1 - side, EDGE + second - 1 : EDGE + second - 1 + pitch, :]
            .astype(jnp.bfloat16)
            .reshape(halves, 16, LANES)
            for second in range(3)
        ]
        for side in range(2)
    ]

    def product(side, row, second):
        line = jnp.broadcast_to(near_ref[side, pl.ds(row, 1), :], (16, LANES)).astype(jnp.bfloat16)
        return (line[None] * shifted[side][second]).reshape(pitch, LANES)

    def build_first(index):
        for side in range(2):
            for parity in range(2):
                for second in range(3):
                    value = product(side, base - 1 + 2 * index + parity, second)
                    lane = parity * GROUP + second * LANES
                    stacked[side, span_of(index * pitch, pitch), lane : lane + LANES] = jnp.maximum(
                        value, jnp.zeros_like(value)
                    )

    def store_first(index, accs):
        for side in range(2):
            for step, pixels, lanes in outputs(n0, pitch, 1):
                row = base + 2 * n0 * index + step
                old = product(side, row, 1).astype(jnp.float32)
                value = old + accs[side][pixels, lanes] + biases[0]
                state[side, at_row(row), :] = masked(rounded(value), row)

    pipeline(
        groups,
        n0,
        build_first,
        lambda index: [convolved(side, side, index, n0, pitch) for side in range(2)],
        store_first,
        1,
    )

    base1, spread1 = 4, 2
    groups1 = (frame - 2 * base1) // (2 * spread1)
    chunk1 = spread1 * pitch
    n1 = share(groups1, chunk1)

    def build_second(index):
        for side in range(2):
            for parity in range(2):
                for e in range(spread1):
                    row = base1 - spread1 + (2 * index + parity) * spread1 + e
                    at = span_of(index * chunk1 + e * pitch, pitch)
                    for second in range(3):
                        begin = EDGE + row * pitch + (second - 1) * spread1
                        value = jnp.maximum(state[side, pl.ds(begin, pitch), :], 0.0)
                        lane = parity * GROUP + second * LANES
                        stacked[apart + side, at, lane : lane + LANES] = value.astype(jnp.bfloat16)

    def store_second(index, accs):
        for step, pixels, lanes in outputs(n1, chunk1, spread1):
            row = base1 + 2 * n1 * spread1 * index + step
            both = [
                rounded(state[side, at_row(row), :] + accs[side][pixels, lanes] + biases[1])
                for side in range(2)
            ]
            state[2, at_row(row), :] = masked(rounded((both[0] + both[1]) * 0.5), row)

    pipeline(
        groups1,
        n1,
        build_second,
        lambda index: [convolved(apart + side, 2 + side, index, n1, chunk1) for side in range(2)],
        store_second,
        2,
    )

    base2, spread2 = EDGE, 4
    groups2 = tile_rows // (2 * spread2)
    chunk2 = spread2 * tile_cols
    n2 = share(groups2, chunk2)

    def build_third(index):
        for parity in range(2):
            for e in range(spread2):
                row = base2 - spread2 + (2 * index + parity) * spread2 + e
                at = span_of(index * chunk2 + e * tile_cols, tile_cols)
                for second in range(3):
                    begin = 2 * EDGE + row * pitch + (second - 1) * spread2
                    value = jnp.maximum(state[2, pl.ds(begin, tile_cols), :], 0.0)
                    lane = parity * GROUP + second * LANES
                    stacked[0, at, lane : lane + LANES] = value.astype(jnp.bfloat16)

    def store_third(index, acc):
        for step, pixels, lanes in outputs(n2, chunk2, spread2):
            row = 2 * n2 * spread2 * index + step
            begin = span_of(2 * EDGE + (base2 + row) * pitch, tile_cols, 8)
            value = state[2, begin, :] + acc[pixels, lanes] + biases[2]
            result[pl.ds(row, channels, stride=tile_rows), :] = value.T[:channels]

    pipeline(groups2, n2, build_third, lambda index: convolved(0, 4, index, n2, chunk2), store_third, 3)
    out_ref[...] = result[...].reshape(channels, tile_rows, tile_cols).astype(jnp.bfloat16)

    def sent(step, carry):
        @pl.when(uses(me, ahead(step)))
        def _():
            copy(step).wait_send()

        return carry

    lax.fori_loop(1, count, sent, 0)


def shards(bins, row_proj, col_proj, conv_weight, conv_bias):
    rows = lax.axis_size("row")
    cols = lax.axis_size("col")
    reps = lax.axis_size("rep")
    own = conv_bias.shape[1]
    if reps > 1:
        row_proj = lax.all_gather(row_proj, "rep", axis=0, tiled=True)
        col_proj = lax.all_gather(col_proj, "rep", axis=0, tiled=True)
        conv_weight = lax.all_gather(conv_weight, "rep", axis=2, tiled=True)
        conv_bias = lax.all_gather(conv_bias, "rep", axis=1, tiled=True)
    span = bins.shape[0]
    count = rows * cols
    total = span * count
    tile_rows = total // rows
    tile_cols = total // cols
    channels = conv_bias.shape[1]
    frame = tile_rows + 2 * EDGE
    pitch = tile_cols + 2 * EDGE
    stack = frame // 2 * pitch * PAIR * 2
    operands = (bins, row_proj, col_proj, conv_weight, conv_bias)
    out = pl.pallas_call(
        functools.partial(decoder, rows, cols),
        out_shape=pltpu.VMEM((channels, tile_rows, tile_cols), jnp.bfloat16),
        in_specs=[pl.BlockSpec(memory_space=pltpu.MemorySpace.HBM)] * 5,
        out_specs=pl.BlockSpec(memory_space=pltpu.VMEM),
        scratch_shapes=[pltpu.VMEM(x.shape, x.dtype) for x in operands]
        + [
            pltpu.VMEM((count, 2 * span, LANES), jnp.bfloat16),
            pltpu.VMEM((2, frame, LANES), jnp.float32),
            pltpu.VMEM((2, pitch + 2 * EDGE, LANES), jnp.float32),
            pltpu.VMEM((3, frame * pitch + 2 * EDGE, LANES), jnp.float32),
            pltpu.VMEM((4 if 4 * stack <= SPARE else 2, frame // 2 * pitch, PAIR), jnp.bfloat16),
            pltpu.VMEM((5, 2 * PAIR, 2 * LANES), jnp.bfloat16),
            pltpu.VMEM((channels * tile_rows, tile_cols), jnp.float32),
            pltpu.SemaphoreType.DMA((5,)),
            pltpu.SemaphoreType.DMA((count,)),
            pltpu.SemaphoreType.DMA((count,)),
        ],
        compiler_params=pltpu.CompilerParams(
            collective_id=0, has_side_effects=True, vmem_limit_bytes=60 * 2**20
        ),
        name="decode_map",
    )(*operands)
    if reps > 1:
        out = lax.dynamic_slice_in_dim(out, lax.axis_index("rep") * own, own, 0)
    return out


def solution(mesh):
    placed = (
        P(("groups", "row", "col"), None),
        P("rep", None),
        P("rep", None),
        P(None, None, "rep", None),
        P(None, "rep"),
    )
    return jax.shard_map(
        shards,
        mesh=mesh,
        in_specs=placed,
        out_specs=P("rep", ("groups", "row"), "col"),
        check_vma=False,
    )
```

```python
import functools

import jax
import jax.numpy as jnp
from jax import lax
from jax.experimental import pallas as pl
from jax.experimental.pallas import tpu as pltpu
from jax.sharding import PartitionSpec as P

MESH = pl.DeviceIdType.MESH
EDGE = 8
LANES = 128
GROUP = 3 * LANES
PAIR = 2 * GROUP
NT = (((1,), (1,)), ((), ()))
ROWS_PER_DOT = 512
MOST_CHUNKS = 16
SPARE = 24 * 2**20


def rounded(value):
    return value.astype(jnp.bfloat16).astype(jnp.float32)


def share(groups, chunk):
    return max(n for n in range(1, groups + 1) if groups % n == 0 and (n == 1 or n * chunk <= ROWS_PER_DOT))


def decoder(
    rows,
    cols,
    bins_hbm,
    rp_hbm,
    cp_hbm,
    w_hbm,
    b_hbm,
    out_ref,
    bins_ref,
    rp_ref,
    cp_ref,
    w_ref,
    b_ref,
    held,
    near_ref,
    far_ref,
    state,
    stacked,
    packed,
    result,
    load_sem,
    send_sem,
    recv_sem,
):
    count = rows * cols
    row_index = lax.axis_index("row")
    col_index = lax.axis_index("col")
    me = row_index * cols + col_index
    span, channels = bins_ref.shape[0], rp_ref.shape[0]
    total = span * count
    _, tile_rows, tile_cols = out_ref.shape
    pitch = tile_cols + 2 * EDGE
    frame = tile_rows + 2 * EDGE
    apart = stacked.shape[0] - 2

    loads = [
        pltpu.make_async_copy(source, target, load_sem.at[i])
        for i, (source, target) in enumerate(
            [(bins_hbm, bins_ref), (rp_hbm, rp_ref), (cp_hbm, cp_ref), (w_hbm, w_ref), (b_hbm, b_ref)]
        )
    ]
    for load in loads:
        load.start()

    def uses(row, col, block):
        near_block = row * (tile_rows // span)
        far_block = col * (tile_cols // span)
        return ((block >= near_block - 1) & (block <= near_block + tile_rows // span)) | (
            (block >= far_block - 1) & (block <= far_block + tile_cols // span)
        )

    def around(visit, start):
        def one(step, carry):
            row = row_index + step
            row = jnp.where(row >= rows, row - rows, row)
            for col in range(cols):
                carry = visit(row, col, row * cols + col, carry)
            return carry

        return lax.fori_loop(0, rows, one, start)

    def sends_to(row, col, other):
        return (other != me) & uses(row, col, me)

    def comes_from(other):
        return (other != me) & uses(row_index, col_index, other)

    barrier = pltpu.get_barrier_semaphore()

    def greet(row, col, other, targets):
        @pl.when(comes_from(other))
        def _():
            pl.semaphore_signal(
                barrier, inc=1, device_id={"row": row, "col": col}, device_id_type=MESH
            )

        return targets + jnp.where(sends_to(row, col, other), 1, 0)

    targets = around(greet, 0)
    near_ref[...] = jnp.zeros_like(near_ref)
    far_ref[...] = jnp.zeros_like(far_ref)
    packed[...] = jnp.zeros_like(packed)
    for load in loads[:3]:
        load.wait()
    bins = bins_ref[...]
    terms = [
        lax.dot_general(bins, ref[...], NT, preferred_element_type=jnp.float32)
        for ref in (rp_ref, cp_ref)
    ]
    blank = jnp.zeros((2 * span, LANES - channels), jnp.float32)
    held[me] = jnp.concatenate([jnp.concatenate(terms, axis=0), blank], axis=1).astype(jnp.bfloat16)
    pl.semaphore_wait(barrier, targets)

    def copy(row, col, target, source):
        return pltpu.make_async_remote_copy(
            src_ref=held.at[me],
            dst_ref=held.at[me],
            send_sem=send_sem.at[target],
            recv_sem=recv_sem.at[source],
            device_id={"row": row, "col": col},
            device_id_type=MESH,
        )

    def send(row, col, other, carry):
        @pl.when(sends_to(row, col, other))
        def _():
            copy(row, col, other, me).start()

        return carry

    around(send, 0)

    for load in loads[3:]:
        load.wait()
    def pack(layer, tap):
        filters = w_ref[layer, tap].astype(jnp.float32).T.astype(jnp.bfloat16)
        for swapped in range(2 if layer < 2 else 1):
            first, second = (tap % 3, tap // 3) if swapped else (tap // 3, tap % 3)
            for parity in range(2):
                at = (first + parity) * GROUP + second * LANES
                packed[
                    2 * layer + swapped,
                    at : at + channels,
                    parity * LANES : parity * LANES + channels,
                ] = filters

    for tap in range(9):
        pack(0, tap)
    fill = jnp.zeros((1, LANES - channels), jnp.float32)
    biases = [jnp.concatenate([b_ref[l : l + 1, :], fill], axis=1) for l in range(3)]

    def finish(row, col, other, carry):
        @pl.when(comes_from(other))
        def _():
            copy(row, col, other, other).wait_recv()

        return carry

    around(finish, 0)

    def lay(out, first, blocks, offset):
        def one(index, carry):
            block = first + index

            @pl.when((block >= 0) & (block < count))
            def _():
                values = held[block].astype(jnp.float32)
                at = pl.ds(pl.multiple_of(offset + index * span, 8), span)
                out[0, at, :] = values[:span]
                out[1, at, :] = values[span:]

            return carry

        lax.fori_loop(0, blocks, one, 0)

    lay(near_ref, row_index * (tile_rows // span) - 1, frame // span, 0)
    lay(far_ref, col_index * (tile_cols // span) - 1, pitch // span, EDGE)

    cells = lax.broadcasted_iota(jnp.int32, (pitch, LANES), 0)
    edge_cells = cells[:EDGE]
    from_left = jnp.where(col_index > 0, 0, EDGE)
    to_right = jnp.where(col_index < cols - 1, EDGE, 0)
    from_top = jnp.where(row_index > 0, 0, pitch)
    from_bottom = jnp.where(row_index < rows - 1, 0, pitch)

    def masked(value, row):
        left = jnp.where(edge_cells >= from_left, value[:EDGE], 0.0)
        right = jnp.where(edge_cells < to_right, value[-EDGE:], 0.0)
        value = jnp.concatenate([left, value[EDGE:-EDGE], right], axis=0)
        if isinstance(row, int):
            if row < EDGE:
                value = jnp.where(cells >= from_top, value, 0.0)
            elif row >= EDGE + tile_rows:
                value = jnp.where(cells >= from_bottom, value, 0.0)
            return value
        start = jnp.where(row < EDGE, from_top, jnp.where(row >= EDGE + tile_rows, from_bottom, 0))
        return jnp.where(cells >= start, value, 0.0)

    def span_of(begin, size, unit=16):
        return pl.ds(begin if isinstance(begin, int) else pl.multiple_of(begin, unit), size)

    def at_row(row):
        return span_of(EDGE + row * pitch, pitch, 8)

    def convolved(side, slot, index, n, chunk):
        here = span_of(index * (n * chunk), n * chunk)
        after = span_of(index * (n * chunk) + chunk, n * chunk)
        return jnp.dot(
            jnp.concatenate([stacked[side, here, :], stacked[side, after, :]], axis=1),
            packed[slot],
            preferred_element_type=jnp.float32,
        )

    def outputs(n, chunk, spread):
        width = chunk // spread
        for group in range(n):
            for parity in range(2):
                for e in range(spread):
                    begin = group * chunk + e * width
                    yield (
                        (2 * group + parity) * spread + e,
                        slice(begin, begin + width),
                        slice(parity * LANES, (parity + 1) * LANES),
                    )

    def pipeline(groups, n, build, multiply, store, later):
        chunks = groups // n
        pending = [(later, tap) for tap in range(9)] if later < 3 else []
        quota = -(-len(pending) // chunks)
        if chunks > MOST_CHUNKS:
            for item in pending:
                pack(*item)
            lax.fori_loop(0, groups + 1, lambda i, c: (build(i), c)[1], 0)
            lax.fori_loop(0, chunks, lambda i, c: (store(i, multiply(i)), c)[1], 0)
            return
        for i in range(n + 1):
            build(i)
        held_acc = None
        for i in range(chunks):
            acc = multiply(i)
            for item in pending[i * quota : (i + 1) * quota]:
                pack(*item)
            if i + 1 < chunks:
                for j in range(n):
                    build((i + 1) * n + 1 + j)
            if held_acc is not None:
                store(i - 1, held_acc)
            held_acc = acc
        store(chunks - 1, held_acc)

    base = 2
    groups = (frame - 2 * base) // 2
    n0 = share(groups, pitch)
    halves = pitch // 16
    shifted = [
        [
            far_ref[1 - side, EDGE + second - 1 : EDGE + second - 1 + pitch, :]
            .astype(jnp.bfloat16)
            .reshape(halves, 16, LANES)
            for second in range(3)
        ]
        for side in range(2)
    ]

    def product(side, row, second):
        line = jnp.broadcast_to(near_ref[side, pl.ds(row, 1), :], (16, LANES)).astype(jnp.bfloat16)
        return (line[None] * shifted[side][second]).reshape(pitch, LANES)

    def build_first(index):
        for side in range(2):
            for parity in range(2):
                for second in range(3):
                    value = product(side, base - 1 + 2 * index + parity, second)
                    lane = parity * GROUP + second * LANES
                    stacked[side, span_of(index * pitch, pitch), lane : lane + LANES] = jnp.maximum(
                        value, jnp.zeros_like(value)
                    )

    def store_first(index, accs):
        for side in range(2):
            for step, pixels, lanes in outputs(n0, pitch, 1):
                row = base + 2 * n0 * index + step
                old = product(side, row, 1).astype(jnp.float32)
                value = old + accs[side][pixels, lanes] + biases[0]
                state[side, at_row(row), :] = masked(rounded(value), row)

    pipeline(
        groups,
        n0,
        build_first,
        lambda index: [convolved(side, side, index, n0, pitch) for side in range(2)],
        store_first,
        1,
    )

    base1, spread1 = 4, 2
    groups1 = (frame - 2 * base1) // (2 * spread1)
    chunk1 = spread1 * pitch
    n1 = share(groups1, chunk1)

    def build_second(index):
        for side in range(2):
            for parity in range(2):
                for e in range(spread1):
                    row = base1 - spread1 + (2 * index + parity) * spread1 + e
                    at = span_of(index * chunk1 + e * pitch, pitch)
                    for second in range(3):
                        begin = EDGE + row * pitch + (second - 1) * spread1
                        value = jnp.maximum(state[side, pl.ds(begin, pitch), :], 0.0)
                        lane = parity * GROUP + second * LANES
                        stacked[apart + side, at, lane : lane + LANES] = value.astype(jnp.bfloat16)

    def store_second(index, accs):
        for step, pixels, lanes in outputs(n1, chunk1, spread1):
            row = base1 + 2 * n1 * spread1 * index + step
            both = [
                rounded(state[side, at_row(row), :] + accs[side][pixels, lanes] + biases[1])
                for side in range(2)
            ]
            state[2, at_row(row), :] = masked(rounded((both[0] + both[1]) * 0.5), row)

    pipeline(
        groups1,
        n1,
        build_second,
        lambda index: [convolved(apart + side, 2 + side, index, n1, chunk1) for side in range(2)],
        store_second,
        2,
    )

    base2, spread2 = EDGE, 4
    groups2 = tile_rows // (2 * spread2)
    chunk2 = spread2 * tile_cols
    n2 = share(groups2, chunk2)

    def build_third(index):
        for parity in range(2):
            for e in range(spread2):
                row = base2 - spread2 + (2 * index + parity) * spread2 + e
                at = span_of(index * chunk2 + e * tile_cols, tile_cols)
                for second in range(3):
                    begin = 2 * EDGE + row * pitch + (second - 1) * spread2
                    value = jnp.maximum(state[2, pl.ds(begin, tile_cols), :], 0.0)
                    lane = parity * GROUP + second * LANES
                    stacked[0, at, lane : lane + LANES] = value.astype(jnp.bfloat16)

    def store_third(index, acc):
        for step, pixels, lanes in outputs(n2, chunk2, spread2):
            row = 2 * n2 * spread2 * index + step
            begin = span_of(2 * EDGE + (base2 + row) * pitch, tile_cols, 8)
            value = state[2, begin, :] + acc[pixels, lanes] + biases[2]
            result[pl.ds(row, channels, stride=tile_rows), :] = value.T[:channels]

    pipeline(groups2, n2, build_third, lambda index: convolved(0, 4, index, n2, chunk2), store_third, 3)
    out_ref[...] = result[...].reshape(channels, tile_rows, tile_cols).astype(jnp.bfloat16)

    def sent(row, col, other, carry):
        @pl.when(sends_to(row, col, other))
        def _():
            copy(row, col, other, me).wait_send()

        return carry

    around(sent, 0)


def shards(bins, row_proj, col_proj, conv_weight, conv_bias):
    rows = lax.axis_size("row")
    cols = lax.axis_size("col")
    reps = lax.axis_size("rep")
    own = conv_bias.shape[1]
    if reps > 1:
        row_proj = lax.all_gather(row_proj, "rep", axis=0, tiled=True)
        col_proj = lax.all_gather(col_proj, "rep", axis=0, tiled=True)
        conv_weight = lax.all_gather(conv_weight, "rep", axis=2, tiled=True)
        conv_bias = lax.all_gather(conv_bias, "rep", axis=1, tiled=True)
    span = bins.shape[0]
    count = rows * cols
    total = span * count
    tile_rows = total // rows
    tile_cols = total // cols
    channels = conv_bias.shape[1]
    frame = tile_rows + 2 * EDGE
    pitch = tile_cols + 2 * EDGE
    stack = frame // 2 * pitch * PAIR * 2
    operands = (bins, row_proj, col_proj, conv_weight, conv_bias)
    out = pl.pallas_call(
        functools.partial(decoder, rows, cols),
        out_shape=pltpu.VMEM((channels, tile_rows, tile_cols), jnp.bfloat16),
        in_specs=[pl.BlockSpec(memory_space=pltpu.MemorySpace.HBM)] * 5,
        out_specs=pl.BlockSpec(memory_space=pltpu.VMEM),
        scratch_shapes=[pltpu.VMEM(x.shape, x.dtype) for x in operands]
        + [
            pltpu.VMEM((count, 2 * span, LANES), jnp.bfloat16),
            pltpu.VMEM((2, frame, LANES), jnp.float32),
            pltpu.VMEM((2, pitch + 2 * EDGE, LANES), jnp.float32),
            pltpu.VMEM((3, frame * pitch + 2 * EDGE, LANES), jnp.float32),
            pltpu.VMEM((4 if 4 * stack <= SPARE else 2, frame // 2 * pitch, PAIR), jnp.bfloat16),
            pltpu.VMEM((5, 2 * PAIR, 2 * LANES), jnp.bfloat16),
            pltpu.VMEM((channels * tile_rows, tile_cols), jnp.float32),
            pltpu.SemaphoreType.DMA((5,)),
            pltpu.SemaphoreType.DMA((count,)),
            pltpu.SemaphoreType.DMA((count,)),
        ],
        compiler_params=pltpu.CompilerParams(
            collective_id=0, has_side_effects=True, vmem_limit_bytes=60 * 2**20
        ),
        name="decode_map",
    )(*operands)
    if reps > 1:
        out = lax.dynamic_slice_in_dim(out, lax.axis_index("rep") * own, own, 0)
    return out


def solution(mesh):
    placed = (
        P(("groups", "row", "col"), None),
        P("rep", None),
        P("rep", None),
        P(None, None, "rep", None),
        P(None, "rep"),
    )
    return jax.shard_map(
        shards,
        mesh=mesh,
        in_specs=placed,
        out_specs=P("rep", ("groups", "row"), "col"),
        check_vma=False,
    )
```

```python
import functools

import jax
import jax.numpy as jnp
from jax import lax
from jax.experimental import pallas as pl
from jax.experimental.pallas import tpu as pltpu
from jax.sharding import PartitionSpec as P

MESH = pl.DeviceIdType.MESH
EDGE = 8
LANES = 128
GROUP = 3 * LANES
PAIR = 2 * GROUP
NT = (((1,), (1,)), ((), ()))
ROWS_PER_DOT = 256
MOST_CHUNKS = 16
SPARE = 24 * 2**20


def rounded(value):
    return value.astype(jnp.bfloat16).astype(jnp.float32)


def share(groups, chunk):
    return max(n for n in range(1, groups + 1) if groups % n == 0 and (n == 1 or n * chunk <= ROWS_PER_DOT))


def decoder(
    rows,
    cols,
    bins_hbm,
    rp_hbm,
    cp_hbm,
    w_hbm,
    b_hbm,
    out_ref,
    bins_ref,
    rp_ref,
    cp_ref,
    w_ref,
    b_ref,
    held,
    near_ref,
    far_ref,
    state,
    stacked,
    packed,
    result,
    load_sem,
    send_sem,
    recv_sem,
):
    count = rows * cols
    row_index = lax.axis_index("row")
    col_index = lax.axis_index("col")
    me = row_index * cols + col_index
    span, channels = bins_ref.shape[0], rp_ref.shape[0]
    total = span * count
    _, tile_rows, tile_cols = out_ref.shape
    pitch = tile_cols + 2 * EDGE
    frame = tile_rows + 2 * EDGE
    apart = stacked.shape[0] - 2

    loads = [
        pltpu.make_async_copy(source, target, load_sem.at[i])
        for i, (source, target) in enumerate(
            [(bins_hbm, bins_ref), (rp_hbm, rp_ref), (cp_hbm, cp_ref), (w_hbm, w_ref), (b_hbm, b_ref)]
        )
    ]
    for load in loads:
        load.start()

    def uses(row, col, block):
        near_block = row * (tile_rows // span)
        far_block = col * (tile_cols // span)
        return ((block >= near_block - 1) & (block <= near_block + tile_rows // span)) | (
            (block >= far_block - 1) & (block <= far_block + tile_cols // span)
        )

    def around(visit, start):
        def one(step, carry):
            row = row_index + step
            row = jnp.where(row >= rows, row - rows, row)
            for col in range(cols):
                carry = visit(row, col, row * cols + col, carry)
            return carry

        return lax.fori_loop(0, rows, one, start)

    def sends_to(row, col, other):
        return (other != me) & uses(row, col, me)

    def comes_from(other):
        return (other != me) & uses(row_index, col_index, other)

    barrier = pltpu.get_barrier_semaphore()

    def greet(row, col, other, targets):
        @pl.when(comes_from(other))
        def _():
            pl.semaphore_signal(
                barrier, inc=1, device_id={"row": row, "col": col}, device_id_type=MESH
            )

        return targets + jnp.where(sends_to(row, col, other), 1, 0)

    targets = around(greet, 0)
    near_ref[...] = jnp.zeros_like(near_ref)
    far_ref[...] = jnp.zeros_like(far_ref)
    packed[...] = jnp.zeros_like(packed)
    for load in loads[:3]:
        load.wait()
    bins = bins_ref[...]
    terms = [
        lax.dot_general(bins, ref[...], NT, preferred_element_type=jnp.float32)
        for ref in (rp_ref, cp_ref)
    ]
    blank = jnp.zeros((2 * span, LANES - channels), jnp.float32)
    held[me] = jnp.concatenate([jnp.concatenate(terms, axis=0), blank], axis=1).astype(jnp.bfloat16)
    pl.semaphore_wait(barrier, targets)

    def copy(row, col, target, source):
        return pltpu.make_async_remote_copy(
            src_ref=held.at[me],
            dst_ref=held.at[me],
            send_sem=send_sem.at[target],
            recv_sem=recv_sem.at[source],
            device_id={"row": row, "col": col},
            device_id_type=MESH,
        )

    def send(row, col, other, carry):
        @pl.when(sends_to(row, col, other))
        def _():
            copy(row, col, other, me).start()

        return carry

    around(send, 0)

    for load in loads[3:]:
        load.wait()
    def pack(layer, tap):
        filters = w_ref[layer, tap].astype(jnp.float32).T.astype(jnp.bfloat16)
        for swapped in range(2 if layer < 2 else 1):
            first, second = (tap % 3, tap // 3) if swapped else (tap // 3, tap % 3)
            for parity in range(2):
                at = (first + parity) * GROUP + second * LANES
                packed[
                    2 * layer + swapped,
                    at : at + channels,
                    parity * LANES : parity * LANES + channels,
                ] = filters

    for tap in range(9):
        pack(0, tap)
    fill = jnp.zeros((1, LANES - channels), jnp.float32)
    biases = [jnp.concatenate([b_ref[l : l + 1, :], fill], axis=1) for l in range(3)]

    def finish(row, col, other, carry):
        @pl.when(comes_from(other))
        def _():
            copy(row, col, other, other).wait_recv()

        return carry

    around(finish, 0)

    def lay(out, first, blocks, offset):
        def one(index, carry):
            block = first + index

            @pl.when((block >= 0) & (block < count))
            def _():
                values = held[block].astype(jnp.float32)
                at = pl.ds(pl.multiple_of(offset + index * span, 8), span)
                out[0, at, :] = values[:span]
                out[1, at, :] = values[span:]

            return carry

        lax.fori_loop(0, blocks, one, 0)

    lay(near_ref, row_index * (tile_rows // span) - 1, frame // span, 0)
    lay(far_ref, col_index * (tile_cols // span) - 1, pitch // span, EDGE)

    cells = lax.broadcasted_iota(jnp.int32, (pitch, LANES), 0)
    edge_cells = cells[:EDGE]
    from_left = jnp.where(col_index > 0, 0, EDGE)
    to_right = jnp.where(col_index < cols - 1, EDGE, 0)
    from_top = jnp.where(row_index > 0, 0, pitch)
    from_bottom = jnp.where(row_index < rows - 1, 0, pitch)

    def masked(value, row):
        left = jnp.where(edge_cells >= from_left, value[:EDGE], 0.0)
        right = jnp.where(edge_cells < to_right, value[-EDGE:], 0.0)
        value = jnp.concatenate([left, value[EDGE:-EDGE], right], axis=0)
        if isinstance(row, int):
            if row < EDGE:
                value = jnp.where(cells >= from_top, value, 0.0)
            elif row >= EDGE + tile_rows:
                value = jnp.where(cells >= from_bottom, value, 0.0)
            return value
        start = jnp.where(row < EDGE, from_top, jnp.where(row >= EDGE + tile_rows, from_bottom, 0))
        return jnp.where(cells >= start, value, 0.0)

    def span_of(begin, size, unit=16):
        return pl.ds(begin if isinstance(begin, int) else pl.multiple_of(begin, unit), size)

    def at_row(row):
        return span_of(EDGE + row * pitch, pitch, 8)

    def convolved(side, slot, index, n, chunk):
        here = span_of(index * (n * chunk), n * chunk)
        after = span_of(index * (n * chunk) + chunk, n * chunk)
        return jnp.dot(
            jnp.concatenate([stacked[side, here, :], stacked[side, after, :]], axis=1),
            packed[slot],
            preferred_element_type=jnp.float32,
        )

    def outputs(n, chunk, spread):
        width = chunk // spread
        for group in range(n):
            for parity in range(2):
                for e in range(spread):
                    begin = group * chunk + e * width
                    yield (
                        (2 * group + parity) * spread + e,
                        slice(begin, begin + width),
                        slice(parity * LANES, (parity + 1) * LANES),
                    )

    def pipeline(groups, n, build, multiply, store, later):
        chunks = groups // n
        pending = [(later, tap) for tap in range(9)] if later < 3 else []
        quota = -(-len(pending) // chunks)
        if chunks > MOST_CHUNKS:
            for item in pending:
                pack(*item)
            lax.fori_loop(0, groups + 1, lambda i, c: (build(i), c)[1], 0)
            lax.fori_loop(0, chunks, lambda i, c: (store(i, multiply(i)), c)[1], 0)
            return
        for i in range(n + 1):
            build(i)
        held_acc = None
        for i in range(chunks):
            acc = multiply(i)
            for item in pending[i * quota : (i + 1) * quota]:
                pack(*item)
            if i + 1 < chunks:
                for j in range(n):
                    build((i + 1) * n + 1 + j)
            if held_acc is not None:
                store(i - 1, held_acc)
            held_acc = acc
        store(chunks - 1, held_acc)

    base = 2
    groups = (frame - 2 * base) // 2
    n0 = share(groups, pitch)
    halves = pitch // 16
    shifted = [
        [
            far_ref[1 - side, EDGE + second - 1 : EDGE + second - 1 + pitch, :]
            .astype(jnp.bfloat16)
            .reshape(halves, 16, LANES)
            for second in range(3)
        ]
        for side in range(2)
    ]

    def product(side, row, second):
        line = jnp.broadcast_to(near_ref[side, pl.ds(row, 1), :], (16, LANES)).astype(jnp.bfloat16)
        return (line[None] * shifted[side][second]).reshape(pitch, LANES)

    def build_first(index):
        for side in range(2):
            for parity in range(2):
                for second in range(3):
                    value = product(side, base - 1 + 2 * index + parity, second)
                    lane = parity * GROUP + second * LANES
                    stacked[side, span_of(index * pitch, pitch), lane : lane + LANES] = jnp.maximum(
                        value, jnp.zeros_like(value)
                    )

    def store_first(index, accs):
        for side in range(2):
            for step, pixels, lanes in outputs(n0, pitch, 1):
                row = base + 2 * n0 * index + step
                old = product(side, row, 1).astype(jnp.float32)
                value = old + accs[side][pixels, lanes] + biases[0]
                state[side, at_row(row), :] = masked(rounded(value), row)

    pipeline(
        groups,
        n0,
        build_first,
        lambda index: [convolved(side, side, index, n0, pitch) for side in range(2)],
        store_first,
        1,
    )

    base1, spread1 = 4, 2
    groups1 = (frame - 2 * base1) // (2 * spread1)
    chunk1 = spread1 * pitch
    n1 = share(groups1, chunk1)

    def build_second(index):
        for side in range(2):
            for parity in range(2):
                for e in range(spread1):
                    row = base1 - spread1 + (2 * index + parity) * spread1 + e
                    at = span_of(index * chunk1 + e * pitch, pitch)
                    for second in range(3):
                        begin = EDGE + row * pitch + (second - 1) * spread1
                        value = jnp.maximum(state[side, pl.ds(begin, pitch), :], 0.0)
                        lane = parity * GROUP + second * LANES
                        stacked[apart + side, at, lane : lane + LANES] = value.astype(jnp.bfloat16)

    def store_second(index, accs):
        for step, pixels, lanes in outputs(n1, chunk1, spread1):
            row = base1 + 2 * n1 * spread1 * index + step
            both = [
                rounded(state[side, at_row(row), :] + accs[side][pixels, lanes] + biases[1])
                for side in range(2)
            ]
            state[2, at_row(row), :] = masked(rounded((both[0] + both[1]) * 0.5), row)

    pipeline(
        groups1,
        n1,
        build_second,
        lambda index: [convolved(apart + side, 2 + side, index, n1, chunk1) for side in range(2)],
        store_second,
        2,
    )

    base2, spread2 = EDGE, 4
    groups2 = tile_rows // (2 * spread2)
    chunk2 = spread2 * tile_cols
    n2 = share(groups2, chunk2)

    def build_third(index):
        for parity in range(2):
            for e in range(spread2):
                row = base2 - spread2 + (2 * index + parity) * spread2 + e
                at = span_of(index * chunk2 + e * tile_cols, tile_cols)
                for second in range(3):
                    begin = 2 * EDGE + row * pitch + (second - 1) * spread2
                    value = jnp.maximum(state[2, pl.ds(begin, tile_cols), :], 0.0)
                    lane = parity * GROUP + second * LANES
                    stacked[0, at, lane : lane + LANES] = value.astype(jnp.bfloat16)

    def store_third(index, acc):
        for step, pixels, lanes in outputs(n2, chunk2, spread2):
            row = 2 * n2 * spread2 * index + step
            begin = span_of(2 * EDGE + (base2 + row) * pitch, tile_cols, 8)
            value = state[2, begin, :] + acc[pixels, lanes] + biases[2]
            result[pl.ds(row, channels, stride=tile_rows), :] = value.T[:channels]

    pipeline(groups2, n2, build_third, lambda index: convolved(0, 4, index, n2, chunk2), store_third, 3)
    out_ref[...] = result[...].reshape(channels, tile_rows, tile_cols).astype(jnp.bfloat16)

    def sent(row, col, other, carry):
        @pl.when(sends_to(row, col, other))
        def _():
            copy(row, col, other, me).wait_send()

        return carry

    around(sent, 0)


def shards(bins, row_proj, col_proj, conv_weight, conv_bias):
    rows = lax.axis_size("row")
    cols = lax.axis_size("col")
    reps = lax.axis_size("rep")
    own = conv_bias.shape[1]
    if reps > 1:
        row_proj = lax.all_gather(row_proj, "rep", axis=0, tiled=True)
        col_proj = lax.all_gather(col_proj, "rep", axis=0, tiled=True)
        conv_weight = lax.all_gather(conv_weight, "rep", axis=2, tiled=True)
        conv_bias = lax.all_gather(conv_bias, "rep", axis=1, tiled=True)
    span = bins.shape[0]
    count = rows * cols
    total = span * count
    tile_rows = total // rows
    tile_cols = total // cols
    channels = conv_bias.shape[1]
    frame = tile_rows + 2 * EDGE
    pitch = tile_cols + 2 * EDGE
    stack = frame // 2 * pitch * PAIR * 2
    operands = (bins, row_proj, col_proj, conv_weight, conv_bias)
    out = pl.pallas_call(
        functools.partial(decoder, rows, cols),
        out_shape=pltpu.VMEM((channels, tile_rows, tile_cols), jnp.bfloat16),
        in_specs=[pl.BlockSpec(memory_space=pltpu.MemorySpace.HBM)] * 5,
        out_specs=pl.BlockSpec(memory_space=pltpu.VMEM),
        scratch_shapes=[pltpu.VMEM(x.shape, x.dtype) for x in operands]
        + [
            pltpu.VMEM((count, 2 * span, LANES), jnp.bfloat16),
            pltpu.VMEM((2, frame, LANES), jnp.float32),
            pltpu.VMEM((2, pitch + 2 * EDGE, LANES), jnp.float32),
            pltpu.VMEM((3, frame * pitch + 2 * EDGE, LANES), jnp.float32),
            pltpu.VMEM((4 if 4 * stack <= SPARE else 2, frame // 2 * pitch, PAIR), jnp.bfloat16),
            pltpu.VMEM((5, 2 * PAIR, 2 * LANES), jnp.bfloat16),
            pltpu.VMEM((channels * tile_rows, tile_cols), jnp.float32),
            pltpu.SemaphoreType.DMA((5,)),
            pltpu.SemaphoreType.DMA((count,)),
            pltpu.SemaphoreType.DMA((count,)),
        ],
        compiler_params=pltpu.CompilerParams(
            collective_id=0, has_side_effects=True, vmem_limit_bytes=60 * 2**20
        ),
        name="decode_map",
    )(*operands)
    if reps > 1:
        out = lax.dynamic_slice_in_dim(out, lax.axis_index("rep") * own, own, 0)
    return out


def solution(mesh):
    placed = (
        P(("groups", "row", "col"), None),
        P("rep", None),
        P("rep", None),
        P(None, None, "rep", None),
        P(None, "rep"),
    )
    return jax.shard_map(
        shards,
        mesh=mesh,
        in_specs=placed,
        out_specs=P("rep", ("groups", "row"), "col"),
        check_vma=False,
    )
```
